512 devices in a mesh: row: 32 (over y, x, core), col: 16 (over z).
Axes of the slice: x: 4, y: 4, z: 16, core: 2. Of those that a mesh axis runs over, the one named last changes fastest.
Arguments:
- matrix: float32 [12288, 12288], P('row', 'col'), may hold values from -10 to 10, as said below
- panel: float32 [12288, 64], P('row'), may hold values from -1.12763724 to 1.12763724
Outputs:
- updated: float32 [12288, 12288], P('row', 'col')
- band_block: float32 [64, 64], replicated
The draws below stay inside these ranges and needn't reach their ends.
Inputs may be any that keep to these rules, and one draw needn't show every extreme that they name: matrix is exactly symmetric.
All inputs are finite; a program needn't handle non-finite values.
Results may differ from the reference program's by a relative error of at most 0.0002.
Values sent between devices are 32-bit elements; how exact they have to be, the bound alone decides.
A program may use at most 64 MiB of HBM per device.

```python
import jax
import jax.numpy as jnp
from jax import lax

N = 12288
PANEL_COLUMNS = 64


def draw_matrix(key, part):
    random_part = jax.random.normal(key, (N, N), jnp.float32)
    random_part = jnp.clip(random_part, -5.0, 5.0)
    symmetric = (random_part + random_part.T) * 0.7
    return symmetric


def draw_panel(key, part):
    random_part = jnp.clip(jax.random.normal(key, (N, PANEL_COLUMNS), jnp.float32), -5.0, 5.0)
    row_spread = 2.302
    row_scale = jnp.exp(jax.random.uniform(jax.random.fold_in(key, 1), (N,), jnp.float32, 0.0, row_spread))
    column_scale = jnp.exp(jax.random.uniform(jax.random.fold_in(key, 2), (PANEL_COLUMNS,), jnp.float32, 0.0, 2.302))
    return random_part * row_scale[:, None] * column_scale[None, :] / (4.0 * jnp.sqrt(jnp.float32(N)))


def setup_inputs(seed: int = 0) -> dict:
    splits = jax.random.split(jax.random.key(seed), 3)
    matrix = draw_matrix(jax.random.fold_in(splits[2], 71), 0)
    panel = draw_panel(jax.random.fold_in(splits[2], 71), 0)
    return dict(matrix=matrix, panel=panel)


precise = lax.Precision.HIGHEST

def reference(matrix, panel):
    row_number = jnp.arange(N)
    column_position = jnp.arange(PANEL_COLUMNS)

    def householder_column(current_column_index, iteration_state):
        reduced_matrix, householder_vectors, householder_scales = iteration_state
        column = lax.optimization_barrier(jnp.sum(jnp.where(column_position[None, :] == current_column_index, reduced_matrix, 0.0), axis=1))
        leading = jnp.sum(jnp.where(row_number == current_column_index, column, 0.0))
        length = jnp.sqrt(jnp.sum(jnp.where(row_number >= current_column_index, column * column, 0.0)))
        shifted = leading + length
        vector = jnp.where(row_number > current_column_index, column / shifted, 0.0) + jnp.where(row_number == current_column_index, 1.0, 0.0)
        householder_scale = shifted / length
        projected = jnp.dot(vector, reduced_matrix, precision=precise)
        reduced_matrix = reduced_matrix - householder_scale * vector[:, None] * projected[None, :]
        householder_vectors = jnp.where(column_position[None, :] == current_column_index, vector[:, None], householder_vectors)
        householder_scales = jnp.where(column_position == current_column_index, householder_scale, householder_scales)
        return (reduced_matrix, householder_vectors, householder_scales)
    initial_state = (panel, jnp.zeros((N, PANEL_COLUMNS), jnp.float32), jnp.zeros((PANEL_COLUMNS,), jnp.float32))
    reduced_matrix, householder_vectors, householder_scales = lax.fori_loop(0, PANEL_COLUMNS, householder_column, initial_state)
    band_block = jnp.triu(reduced_matrix[:PANEL_COLUMNS])
    correlation = jnp.dot(householder_vectors.T, householder_vectors, precision=precise)

    def extend_triangle(current_column_index, triangle):
        householder_scale = jnp.sum(jnp.where(column_position == current_column_index, householder_scales, 0.0))
        wanted = lax.optimization_barrier(jnp.sum(jnp.where(column_position[None, :] == current_column_index, correlation, 0.0), axis=1))
        new_column = -householder_scale * jnp.dot(triangle, wanted, precision=precise)
        new_column = jnp.where(column_position < current_column_index, new_column, 0.0) + jnp.where(column_position == current_column_index, householder_scale, 0.0)
        return jnp.where(column_position[None, :] == current_column_index, new_column[:, None], triangle)
    triangle = lax.fori_loop(0, PANEL_COLUMNS, extend_triangle, jnp.zeros((PANEL_COLUMNS, PANEL_COLUMNS), jnp.float32))
    product = jnp.dot(matrix, householder_vectors, precision=precise)
    applied = jnp.dot(product, triangle, precision=precise)
    coupling = jnp.dot(triangle.T, jnp.dot(householder_vectors.T, applied, precision=precise), precision=precise)
    corrected = applied - 0.5 * jnp.dot(householder_vectors, coupling, precision=precise)
    left_factor = jnp.concatenate([householder_vectors, corrected], 1)
    right_factor = jnp.concatenate([corrected, householder_vectors], 1)
    updated = matrix - jnp.dot(left_factor, right_factor.T, precision=precise)
    return (updated, band_block)
```

```python
import jax
import jax.numpy as jnp
from jax import lax
from jax.experimental import pallas as pl
from jax.experimental.pallas import tpu as pltpu
from jax.sharding import PartitionSpec as P

F32 = jnp.float32
precise = lax.Precision.HIGHEST
ROWS, COLS, WIDTH = 384, 768, 64
PIECE = 24


def mm(a, b, ca=1, cb=0):
    return lax.dot_general(
        a, b, (((ca,), (cb,)), ((), ())), precision=precise, preferred_element_type=F32
    )


def spot(i):
    return (i % 4) * 4 + i // 4


def loop(lo, hi, step):
    lax.fori_loop(lo, hi, lambda i, carry: (step(i), carry)[1], 0)


def fold(block):
    return jnp.concatenate([block[:32], block[32:]], axis=1)


def unfold(block):
    return jnp.concatenate([block[:, :64], block[:, 64:]], axis=0)


def gather_kernel(
    a_hbm, p_hbm, band_ref, left_ref, dzb_ref, dp_ref,
    a_ref, p_ref, pe_ref, t_ref, t1_ref, tr_ref, zb_ref, zbr_ref, pp_ref,
    dzb, dp,
    gh_ref, gh1_ref, gr_ref, gx_ref, hx_ref, gs_ref,
    j_ref, j1_ref, jr_ref, jx_ref,
    gk, hh, ln, rk, lno,
    load_sem, one_send, one_recv,
    gs_sem, gr_sem, hs_sem, ts_sem, tr_sem, ps_sem, pr_sem, ds_sem, dr_sem,
    js_sem, jr_sem, us_sem, ur_sem, vs_sem, vr_sem,
):
    row = lax.axis_index("row")
    col = lax.axis_index("col")
    chip = row // 2
    core = row % 2
    other = 1 - core
    near = (chip * 2 + other, col)
    swap = (col * 2 + core, chip)

    load_p = pltpu.make_async_copy(p_hbm, p_ref, load_sem.at[0])
    load_a = pltpu.make_async_copy(a_hbm, a_ref, load_sem.at[1])
    load_p.start()
    load_a.start()

    def peer(d):
        return (chip + d) % 16

    def plane(i):
        return (i * 2 + core, col)

    def remote(src, dst, send, recv, device):
        return pltpu.make_async_remote_copy(
            src_ref=src, dst_ref=dst, send_sem=send, recv_sem=recv,
            device_id=device, device_id_type=pl.DeviceIdType.MESH,
        )

    def far(d):
        return (col % 4) + 4 * ((col // 4 + d) % 4)

    def close(d):
        return 4 * (col // 4) + (col % 4 + d) % 4

    barrier = pltpu.get_barrier_semaphore()

    def greet(device):
        pl.semaphore_signal(
            barrier, inc=1, device_id=device, device_id_type=pl.DeviceIdType.MESH
        )

    greet(near)
    loop(1, 16, lambda d: greet(plane(peer(d))))
    loop(1, 4, lambda d: greet((row, far(d))))
    loop(1, 4, lambda d: greet((row, close(d))))

    @pl.when(chip != col)
    def _():
        greet(swap)

    load_p.wait()
    panel = p_ref[...]
    rows_at = lax.broadcasted_iota(jnp.int32, (ROWS, WIDTH), 0)
    lanes_at = lax.broadcasted_iota(jnp.int32, (ROWS, WIDTH), 1)
    is_first = (row == 0).astype(F32)
    unit = jnp.where(rows_at == lanes_at, is_first, 0.0)
    pe_ref[...] = jnp.concatenate([panel, unit], axis=1)
    gram = mm(panel, panel, 0, 0)
    gh_ref[0] = fold(gram)
    gh_ref[1] = fold(panel[:WIDTH]) * is_first

    @pl.when(chip != col)
    def _():
        pl.semaphore_wait(barrier, 23)

    @pl.when(chip == col)
    def _():
        pl.semaphore_wait(barrier, 22)

    send_gh = remote(gh_ref, gh1_ref, one_send.at[0], one_recv.at[0], near)
    send_gh.start()

    send_pp = remote(
        p_ref.at[pl.ds(pl.multiple_of(PIECE * spot(col), 8), PIECE)],
        pp_ref, one_send.at[1], one_recv.at[1], swap,
    )
    keep_pp = pltpu.make_async_copy(
        p_ref.at[pl.ds(pl.multiple_of(PIECE * spot(col), 8), PIECE)], pp_ref, load_sem.at[2]
    )

    @pl.when(chip != col)
    def _():
        send_pp.start()

    @pl.when(chip == col)
    def _():
        keep_pp.start()

    load_a.wait()
    pe = pe_ref[...]
    for b in range(3):
        t_ref[256 * b : 256 * b + 256] = mm(a_ref[:, 256 * b : 256 * b + 256], pe, 0, 0)

    send_t = remote(
        t_ref.at[pl.ds(pl.multiple_of(other * ROWS, 8), ROWS)],
        t1_ref, one_send.at[2], one_recv.at[2], near,
    )
    send_t.start()

    send_gh.wait_recv()
    half = pl.ds(pl.multiple_of(core * 16, 8), 16)
    gs_ref[0] = gh_ref[0, half] + gh1_ref[0, half]
    gs_ref[1] = gh_ref[1, half] + gh1_ref[1, half]
    gr_ref[chip] = gs_ref[0]

    def send_gram(d):
        i = peer(d)
        remote(gs_ref.at[0], gr_ref.at[chip], gs_sem.at[i], gr_sem.at[chip], plane(i)).start()

    def send_head(d):
        i = peer(d)
        remote(gs_ref.at[1], hx_ref, hs_sem.at[i], one_recv.at[3], plane(i)).start()

    loop(1, 16, send_gram)

    @pl.when(chip == 0)
    def _():
        loop(1, 16, send_head)

    send_t.wait_recv()
    mine = pl.multiple_of(core * ROWS, 8)
    t_ref[pl.ds(mine, ROWS)] = t_ref[pl.ds(mine, ROWS)] + t1_ref[...]

    def t_piece(i):
        return t_ref.at[pl.ds(pl.multiple_of(core * ROWS + PIECE * spot(i), 8), PIECE)]

    def send_piece(d):
        i = peer(d)
        remote(t_piece(i), tr_ref.at[chip], ts_sem.at[i], tr_sem.at[chip], plane(i)).start()

    loop(1, 16, send_piece)
    tr_ref[chip] = t_ref[pl.ds(pl.multiple_of(core * ROWS + PIECE * spot(chip), 8), PIECE)]

    @pl.when(chip != col)
    def _():
        send_pp.wait_recv()

    @pl.when(chip == col)
    def _():
        keep_pp.wait()

    def place(i):
        return pl.ds(pl.multiple_of(core * ROWS + PIECE * spot(i), 8), PIECE)

    def send_rows(d):
        i = peer(d)
        remote(pp_ref, dp.at[place(chip)], ps_sem.at[i], pr_sem.at[chip], plane(i)).start()

    loop(1, 16, send_rows)
    dp[place(chip)] = pp_ref[...]

    def wait_gram(d):
        i = peer(d)
        remote(gs_ref.at[0], gr_ref.at[i], gs_sem.at[i], gr_sem.at[i], plane(i)).wait_recv()

    loop(1, 16, wait_gram)
    total = gr_ref[0]
    for i in range(1, 16):
        total = total + gr_ref[i]

    @pl.when(chip != 0)
    def _():
        remote(gs_ref.at[1], hx_ref, hs_sem.at[0], one_recv.at[3], plane(0)).wait_recv()

    @pl.when(chip == 0)
    def _():
        hx_ref[...] = gs_ref[1]

    gx_ref[0, half] = total
    gx_ref[1, half] = hx_ref[...]
    send_gx = remote(
        gx_ref.at[:, half], gx_ref.at[:, half], one_send.at[4], one_recv.at[4], near
    )
    send_gx.start()
    send_gx.wait_recv()

    gram = unfold(gx_ref[0])
    head = unfold(gx_ref[1])
    eye = jnp.where(
        lax.broadcasted_iota(jnp.int32, (64, 64), 0)
        == lax.broadcasted_iota(jnp.int32, (64, 64), 1), 1.0, 0.0,
    )
    gk[...] = jnp.concatenate([gram, eye], axis=1)
    hh[...] = jnp.concatenate([head, head.T], axis=1)
    ln[...] = jnp.concatenate([eye, eye], axis=1)

    lane = lax.broadcasted_iota(jnp.int32, (64, 128), 1)
    deep = lax.broadcasted_iota(jnp.int32, (64, 128), 0)
    lane1 = lax.broadcasted_iota(jnp.int32, (1, 128), 1)
    left = lane < 64
    left1 = lane1 < 64

    def column(j):
        at = pl.ds(j, 1)
        g_row, h_row, l_row = gk[at], hh[at], ln[at]
        g, h, l = gk[...], hh[...], ln[...]
        g_col = jnp.sum(jnp.where(lane == j, g, 0.0), axis=1, keepdims=True)
        h_col = jnp.sum(jnp.where(lane == j, h, 0.0), axis=1, keepdims=True)
        m_col = jnp.sum(jnp.where(lane == j + 64, h, 0.0), axis=1, keepdims=True)
        pivot = jnp.sum(jnp.where(lane1 == j, g_row, 0.0), axis=1, keepdims=True)
        entry = jnp.sum(jnp.where(lane1 == j, h_row, 0.0), axis=1, keepdims=True)
        inv = lax.rsqrt(pivot)
        inv = inv * (1.5 - 0.5 * pivot * inv * inv)
        scaled = g_row * inv
        turn = 1.0 / (entry + pivot * inv)
        rk[at] = -scaled
        gk[...] = g - (g_col * inv) * scaled
        factor = jnp.where(left, h_col * turn, m_col + g_col * inv)
        factor = jnp.where(deep > j, factor, 0.0)
        h_line = jnp.where(left1, h_row + scaled, h_row * turn)
        l_line = jnp.where(left1, l_row, l_row * turn)
        lno[at] = l_line
        hh[...] = h - factor * h_line
        ln[...] = l - factor * l_line

    loop(0, 16, column)

    def wait_piece(d):
        i = peer(d)
        remote(t_piece(i), tr_ref.at[i], ts_sem.at[i], tr_sem.at[i], plane(i)).wait_recv()

    loop(1, 16, wait_piece)
    total = tr_ref[0]
    for i in range(1, 16):
        total = total + tr_ref[i]
    zb_ref[...] = total

    def send_product(d):
        i = peer(d)
        remote(zb_ref, dzb.at[place(chip)], ds_sem.at[i], dr_sem.at[chip], plane(i)).start()

    there = pl.ds(pl.multiple_of(PIECE * spot(chip), 8), PIECE)
    here = pl.ds(pl.multiple_of(PIECE * spot(col), 8), PIECE)
    send_zb = remote(zb_ref, zbr_ref.at[there], one_send.at[5], one_recv.at[5], swap)

    @pl.when(chip != col)
    def _():
        send_zb.start()

    @pl.when(chip == col)
    def _():
        zbr_ref[there] = zb_ref[...]

    loop(1, 16, send_product)
    dzb[place(chip)] = zb_ref[...]

    loop(16, 32, column)

    @pl.when(chip != col)
    def _():
        send_zb.wait_recv()

    def send_far(d):
        i = (col // 4 + d) % 4
        remote(
            zbr_ref.at[here], zbr_ref.at[here], us_sem.at[i], ur_sem.at[col // 4], (row, far(d))
        ).start()

    loop(1, 4, send_far)

    loop(32, 48, column)

    def far_spot(i):
        return zbr_ref.at[pl.ds(pl.multiple_of(PIECE * ((col % 4) * 4 + i), 8), PIECE)]

    def wait_far(d):
        i = (col // 4 + d) % 4
        remote(far_spot(i), far_spot(i), us_sem.at[i], ur_sem.at[i], (row, far(d))).wait_recv()

    loop(1, 4, wait_far)

    def quarter(i):
        return zbr_ref.at[pl.ds(pl.multiple_of(4 * PIECE * i, 8), 4 * PIECE)]

    def send_close(d):
        i = (col % 4 + d) % 4
        remote(
            quarter(col % 4), quarter(col % 4), vs_sem.at[i], vr_sem.at[col % 4], (row, close(d))
        ).start()

    loop(1, 4, send_close)

    def wait_rows(d):
        i = peer(d)
        remote(pp_ref, dp.at[place(i)], ps_sem.at[i], pr_sem.at[i], plane(i)).wait_recv()
        remote(zb_ref, dzb.at[place(i)], ds_sem.at[i], dr_sem.at[i], plane(i)).wait_recv()

    loop(1, 16, wait_rows)
    own = pl.ds(mine, ROWS)
    send_dzb = remote(dzb.at[own], dzb.at[own], one_send.at[6], one_recv.at[6], near)
    send_dp = remote(dp.at[own], dp.at[own], one_send.at[7], one_recv.at[7], near)
    send_dzb.start()
    send_dp.start()

    loop(48, 64, column)

    band = jnp.where(
        lax.broadcasted_iota(jnp.int32, (64, 64), 0)
        <= lax.broadcasted_iota(jnp.int32, (64, 64), 1), rk[:, :64], 0.0,
    )
    band_ref[...] = band
    rs = -mm(lno[:, :64], lno[:, 64:], 0, 0)
    s = mm(rk[:, 64:], rs, 0, 0)

    def wait_close(d):
        i = (col % 4 + d) % 4
        remote(quarter(i), quarter(i), vs_sem.at[i], vr_sem.at[i], (row, close(d))).wait_recv()

    loop(1, 4, wait_close)
    first_rows = panel[:WIDTH] - is_first * band
    y = jnp.concatenate([first_rows, panel[WIDTH:]], axis=0)
    begun = mm(zbr_ref[...], jnp.concatenate([s, -rs], axis=0))
    inner = mm(mm(y, s), begun, 0, 0)

    j_ref[...] = fold(inner)
    send_j = remote(j_ref, j1_ref, one_send.at[8], one_recv.at[8], near)
    send_j.start()
    left_ref[:, :128] = jnp.concatenate([mm(y, s, 1, 1), -mm(y, rs, 1, 1)], axis=1)
    send_j.wait_recv()
    jr_ref[chip] = j_ref[half] + j1_ref[half]

    def send_inner(d):
        i = peer(d)
        remote(jr_ref.at[chip], jr_ref.at[chip], js_sem.at[i], jr_sem.at[chip], plane(i)).start()

    def wait_inner(d):
        i = peer(d)
        remote(jr_ref.at[i], jr_ref.at[i], js_sem.at[i], jr_sem.at[i], plane(i)).wait_recv()

    loop(1, 16, send_inner)
    send_dzb.wait_recv()
    send_dp.wait_recv()
    send_dzb.wait_send()
    send_dp.wait_send()
    dzb_ref[...] = dzb[...]
    dp_ref[...] = dp[...]
    loop(1, 16, wait_inner)
    total = jr_ref[0]
    for i in range(1, 16):
        total = total + jr_ref[i]
    jx_ref[half] = total
    send_jx = remote(jx_ref.at[half], jx_ref.at[half], one_send.at[9], one_recv.at[9], near)
    send_jx.start()
    send_jx.wait_recv()
    coupling = unfold(jx_ref[...])
    left_ref[:, 128:] = begun - mm(y, coupling)

    send_gh.wait_send()
    send_t.wait_send()
    send_gx.wait_send()
    send_j.wait_send()
    send_jx.wait_send()

    @pl.when(chip != col)
    def _():
        send_pp.wait_send()
        send_zb.wait_send()

    def sent(d):
        i = peer(d)
        remote(gs_ref.at[0], gr_ref.at[chip], gs_sem.at[i], gr_sem.at[chip], plane(i)).wait_send()
        remote(t_piece(i), tr_ref.at[chip], ts_sem.at[i], tr_sem.at[chip], plane(i)).wait_send()
        remote(pp_ref, dp.at[place(chip)], ps_sem.at[i], pr_sem.at[chip], plane(i)).wait_send()
        remote(zb_ref, dzb.at[place(chip)], ds_sem.at[i], dr_sem.at[chip], plane(i)).wait_send()
        remote(jr_ref.at[chip], jr_ref.at[chip], js_sem.at[i], jr_sem.at[chip], plane(i)).wait_send()

    loop(1, 16, sent)

    @pl.when(chip == 0)
    def _():
        def head_sent(d):
            i = peer(d)
            remote(gs_ref.at[1], hx_ref, hs_sem.at[i], one_recv.at[3], plane(i)).wait_send()

        loop(1, 16, head_sent)

    def z_sent(d):
        i = (col // 4 + d) % 4
        remote(
            zbr_ref.at[here], zbr_ref.at[here], us_sem.at[i], ur_sem.at[i], (row, far(d))
        ).wait_send()
        j = (col % 4 + d) % 4
        remote(
            quarter(col % 4), quarter(col % 4), vs_sem.at[j], vr_sem.at[j], (row, close(d))
        ).wait_send()

    loop(1, 4, z_sent)


def gathered(matrix, panel):
    dma = pltpu.SemaphoreType.DMA
    vmem = pltpu.VMEM
    return pl.pallas_call(
        gather_kernel,
        out_shape=(
            jax.ShapeDtypeStruct((WIDTH, WIDTH), F32),
            jax.ShapeDtypeStruct((ROWS, 192), F32),
            jax.ShapeDtypeStruct((COLS, 128), F32),
            jax.ShapeDtypeStruct((COLS, WIDTH), F32),
        ),
        in_specs=[pl.BlockSpec(memory_space=pl.ANY)] * 2,
        out_specs=[pl.BlockSpec(memory_space=pltpu.VMEM)] * 4,
        scratch_shapes=[
            vmem((ROWS, COLS), F32),
            vmem((ROWS, WIDTH), F32),
            vmem((ROWS, 128), F32),
            vmem((COLS, 128), F32),
            vmem((ROWS, 128), F32),
            vmem((16, PIECE, 128), F32),
            vmem((PIECE, 128), F32),
            vmem((ROWS, 128), F32),
            vmem((PIECE, WIDTH), F32),
            vmem((COLS, 128), F32),
            vmem((COLS, WIDTH), F32),
            vmem((2, 32, 128), F32),
            vmem((2, 32, 128), F32),
            vmem((16, 16, 128), F32),
            vmem((2, 32, 128), F32),
            vmem((16, 128), F32),
            vmem((2, 16, 128), F32),
            vmem((32, 128), F32),
            vmem((32, 128), F32),
            vmem((16, 16, 128), F32),
            vmem((32, 128), F32),
        ]
        + [vmem((64, 128), F32)] * 5
        + [dma((3,)), dma((10,)), dma((10,))]
        + [dma((16,))] * 11
        + [dma((4,))] * 4,
        compiler_params=pltpu.CompilerParams(
            collective_id=0, has_side_effects=True, vmem_limit_bytes=40 * 1024 * 1024
        ),
        cost_estimate=pl.CostEstimate(flops=10**9, bytes_accessed=10**7, transcendentals=0),
    )(matrix, panel)


def update_kernel(a_ref, left_ref, dzb_ref, dp_ref, band_ref, out_ref, band_out):
    first = (lax.axis_index("col") == 0).astype(F32)
    band = band_ref[...]
    band_out[...] = band
    top = dp_ref[:WIDTH] - first * band
    rows = jnp.concatenate([top, dp_ref[WIDTH:]], axis=0)
    right = jnp.concatenate([dzb_ref[...], rows], axis=1)
    left = left_ref[...]
    for b in range(3):
        part = slice(256 * b, 256 * b + 256)
        out_ref[:, part] = a_ref[:, part] - mm(left, right[part], 1, 1)


def body(matrix, panel):
    band, left, dzb, dp = gathered(matrix, panel)
    return pl.pallas_call(
        update_kernel,
        out_shape=(
            jax.ShapeDtypeStruct((ROWS, COLS), F32),
            jax.ShapeDtypeStruct((WIDTH, WIDTH), F32),
        ),
        compiler_params=pltpu.CompilerParams(vmem_limit_bytes=40 * 1024 * 1024),
        cost_estimate=pl.CostEstimate(flops=10**8, bytes_accessed=10**7, transcendentals=0),
    )(matrix, left, dzb, dp, band)


def solution(mesh):
    return jax.shard_map(
        body,
        mesh=mesh,
        in_specs=(P("row", "col"), P("row", None)),
        out_specs=(P("row", "col"), P()),
        check_vma=False,
    )
```

```python
import jax
import jax.numpy as jnp
from jax import lax
from jax.experimental import pallas as pl
from jax.experimental.pallas import tpu as pltpu
from jax.sharding import PartitionSpec as P

F32 = jnp.float32
precise = lax.Precision.HIGHEST
ROWS, COLS, WIDTH = 384, 768, 64
SLAB = 12
HALF = 192


def mm(a, b, ca=1, cb=0):
    return lax.dot_general(
        a, b, (((ca,), (cb,)), ((), ())), precision=precise, preferred_element_type=F32
    )


def loop(lo, hi, step):
    lax.fori_loop(lo, hi, lambda i, carry: (step(i), carry)[1], 0)


def fold(block):
    rows = block.shape[0] // 2
    return jnp.concatenate([block[:rows], block[rows:]], axis=1)


def unfold(block):
    return jnp.concatenate([block[:, :64], block[:, 64:]], axis=0)


def to_slabs(ref, lead, block):
    folded = fold(block)
    for i in range(16):
        ref[lead + i] = folded[SLAB * i : SLAB * i + SLAB]


def from_slabs(ref, lead):
    return unfold(jnp.concatenate([ref[lead + i] for i in range(16)], axis=0))


def gather_kernel(
    a_hbm, p_hbm, band_ref, base_ref, yj_ref, yc_ref,
    a_ref, pt_ref, p3, pp_ref, t3, t1, tr, zs, b3, bs, d3, zr, br,
    gh_ref, gh1_ref, gr_ref, gx_ref, hx_ref, gs_ref,
    j_ref, j1_ref, jr_ref, jx_ref,
    gk, hh, ln, rk, lno,
    load_sem, one_send, one_recv,
    gs_sem, gr_sem, hs_sem, ts_sem, tr_sem, bs_sem,
    zs_sem, zr_sem, ys_sem, yr_sem, js_sem, jr_sem, ds_sem, dr_sem,
):
    row = lax.axis_index("row")
    col = lax.axis_index("col")
    chip = row // 2
    core = row % 2
    other = 1 - core
    near = (chip * 2 + other, col)
    swap = (col * 2 + core, chip)

    loads = [pltpu.make_async_copy(p_hbm, pt_ref, load_sem.at[0])]
    for b in range(3):
        cut = pl.ds(256 * b, 256)
        loads.append(pltpu.make_async_copy(a_hbm.at[:, cut], a_ref.at[:, cut], load_sem.at[1 + b]))
    for load in loads:
        load.start()

    def peer(d):
        return (chip + d) % 16

    def plane(i):
        return (i * 2 + core, col)

    def remote(src, dst, send, recv, device):
        return pltpu.make_async_remote_copy(
            src_ref=src, dst_ref=dst, send_sem=send, recv_sem=recv,
            device_id=device, device_id_type=pl.DeviceIdType.MESH,
        )

    barrier = pltpu.get_barrier_semaphore()

    def greet(device):
        pl.semaphore_signal(
            barrier, inc=1, device_id=device, device_id_type=pl.DeviceIdType.MESH
        )

    loop(1, 16, lambda d: greet((peer(d) * 2 + core, chip)))

    @pl.when(chip != col)
    def _():
        greet((row, chip))

    loop(1, 16, lambda d: greet(plane(peer(d))))
    greet(near)

    loads[0].wait()
    pt = pt_ref[...]
    panel = pt.T
    is_first = (row == 0).astype(F32)
    gh_ref[0] = fold(mm(pt, pt, 1, 1))
    gh_ref[1] = fold(panel[:WIDTH]) * is_first
    to_slabs(p3, 0, panel)
    parts = []
    for b in range(3):
        loads[1 + b].wait()
        parts.append(mm(pt, a_ref[:, 256 * b : 256 * b + 256]).T)
    partial = jnp.concatenate(parts, axis=0)
    to_slabs(t3, 0, partial[:ROWS])
    to_slabs(t3, 16, partial[ROWS:])

    @pl.when(row == 0)
    def _():
        first_columns = a_ref[:WIDTH].T
        to_slabs(b3, 0, first_columns[:ROWS])
        to_slabs(b3, 16, first_columns[ROWS:])

    @pl.when(chip != col)
    def _():
        pl.semaphore_wait(barrier, 32)

    @pl.when(chip == col)
    def _():
        pl.semaphore_wait(barrier, 31)

    send_gh = remote(gh_ref, gh1_ref, one_send.at[0], one_recv.at[0], near)
    send_gh.start()
    send_t = remote(t3.at[pl.ds(other * 16, 16)], t1, one_send.at[2], one_recv.at[2], near)
    send_t.start()

    send_pp = remote(p3.at[col], pp_ref, one_send.at[1], one_recv.at[1], swap)

    @pl.when(chip != col)
    def _():
        send_pp.start()

    send_b = remote(
        b3.at[pl.ds(16, 16)], b3.at[pl.ds(16, 16)], one_send.at[3], one_recv.at[3], near
    )

    @pl.when(row == 0)
    def _():
        send_b.start()

    send_gh.wait_recv()
    half = pl.ds(pl.multiple_of(core * 16, 8), 16)
    gs_ref[0] = gh_ref[0, half] + gh1_ref[0, half]
    gs_ref[1] = gh_ref[1, half] + gh1_ref[1, half]

    def send_gram(d):
        i = peer(d)
        remote(gs_ref.at[0], gr_ref.at[chip], gs_sem.at[i], gr_sem.at[chip], plane(i)).start()

    def send_head(d):
        i = peer(d)
        remote(gs_ref.at[1], hx_ref, hs_sem.at[i], one_recv.at[5], plane(i)).start()

    loop(1, 16, send_gram)

    @pl.when(chip == 0)
    def _():
        loop(1, 16, send_head)

    gr_ref[chip] = gs_ref[0]

    send_t.wait_recv()
    mine = pl.ds(core * 16, 16)
    t3[mine] = t3[mine] + t1[...]

    def send_part(d):
        i = peer(d)
        remote(t3.at[core * 16 + i], tr.at[chip], ts_sem.at[i], tr_sem.at[chip], plane(i)).start()

    loop(1, 16, send_part)
    tr[chip] = t3[core * 16 + chip]

    @pl.when(row == 1)
    def _():
        send_b.wait_recv()

    def send_first(d):
        i = peer(d)
        remote(b3.at[core * 16 + i], bs, bs_sem.at[i], one_recv.at[6], plane(i)).start()

    @pl.when(chip == 0)
    def _():
        loop(1, 16, send_first)
        bs[...] = b3[core * 16]

    def wait_gram(d):
        i = peer(d)
        remote(gs_ref.at[0], gr_ref.at[i], gs_sem.at[i], gr_sem.at[i], plane(i)).wait_recv()

    loop(1, 16, wait_gram)
    total = gr_ref[0]
    for i in range(1, 16):
        total = total + gr_ref[i]

    @pl.when(chip != 0)
    def _():
        remote(gs_ref.at[1], hx_ref, hs_sem.at[0], one_recv.at[5], plane(0)).wait_recv()

    @pl.when(chip == 0)
    def _():
        hx_ref[...] = gs_ref[1]

    gx_ref[0, half] = total
    gx_ref[1, half] = hx_ref[...]
    send_gx = remote(
        gx_ref.at[:, half], gx_ref.at[:, half], one_send.at[4], one_recv.at[4], near
    )
    send_gx.start()

    slot = core * 16 + chip

    def spread(src, dst, send, recv):
        def step(d):
            z = (col + d) % 16
            remote(src, dst.at[chip], send.at[z], recv.at[chip], (col * 2 + core, z)).start()

        loop(1, 16, step)

        @pl.when(chip != col)
        def _():
            step(0)

        @pl.when(chip == col)
        def _():
            dst[chip] = src[...]

    def share(which, src):
        def step(d):
            i = peer(d)
            remote(
                src, d3.at[which, slot], ds_sem.at[which, i], dr_sem.at[which, chip], plane(i)
            ).start()

        loop(1, 16, step)
        d3[which, slot] = src[...]

    def wait_part(d):
        i = peer(d)
        remote(t3.at[core * 16 + i], tr.at[i], ts_sem.at[i], tr_sem.at[i], plane(i)).wait_recv()

    loop(1, 16, wait_part)
    total = tr[0]
    for i in range(1, 16):
        total = total + tr[i]
    zs[...] = total
    spread(zs, zr, zs_sem, zr_sem)

    @pl.when(chip != 0)
    def _():
        remote(b3.at[core * 16], bs, bs_sem.at[0], one_recv.at[6], plane(0)).wait_recv()

    spread(bs, br, ys_sem, yr_sem)
    share(0, zs)
    share(1, bs)

    send_gx.wait_recv()
    gram = unfold(gx_ref[0])
    head = unfold(gx_ref[1])
    eye = jnp.where(
        lax.broadcasted_iota(jnp.int32, (64, 64), 0)
        == lax.broadcasted_iota(jnp.int32, (64, 64), 1), 1.0, 0.0,
    )
    gk[...] = jnp.concatenate([gram, eye], axis=1)
    hh[...] = jnp.concatenate([head, head.T], axis=1)
    ln[...] = jnp.concatenate([eye, eye], axis=1)

    lane = lax.broadcasted_iota(jnp.int32, (64, 128), 1)
    deep = lax.broadcasted_iota(jnp.int32, (64, 128), 0)
    lane1 = lax.broadcasted_iota(jnp.int32, (1, 128), 1)
    left = lane < 64
    left1 = lane1 < 64

    def column(j):
        at = pl.ds(j, 1)
        g_row, h_row, l_row = gk[at], hh[at], ln[at]
        g, h, l = gk[...], hh[...], ln[...]
        g_col = jnp.sum(jnp.where(lane == j, g, 0.0), axis=1, keepdims=True)
        h_col = jnp.sum(jnp.where(lane == j, h, 0.0), axis=1, keepdims=True)
        m_col = jnp.sum(jnp.where(lane == j + 64, h, 0.0), axis=1, keepdims=True)
        pivot = jnp.sum(jnp.where(lane1 == j, g_row, 0.0), axis=1, keepdims=True)
        entry = jnp.sum(jnp.where(lane1 == j, h_row, 0.0), axis=1, keepdims=True)
        inv = lax.rsqrt(pivot)
        inv = inv * (1.5 - 0.5 * pivot * inv * inv)
        scaled = g_row * inv
        turn = 1.0 / (entry + pivot * inv)
        rk[at] = -scaled
        gk[...] = g - (g_col * inv) * scaled
        factor = jnp.where(left, h_col * turn, m_col + g_col * inv)
        factor = jnp.where(deep > j, factor, 0.0)
        h_line = jnp.where(left1, h_row + scaled, h_row * turn)
        l_line = jnp.where(left1, l_row, l_row * turn)
        lno[at] = l_line
        hh[...] = h - factor * h_line
        ln[...] = l - factor * l_line

    loop(0, 24, column)

    @pl.when(chip != col)
    def _():
        send_pp.wait_recv()

    @pl.when(chip == col)
    def _():
        pp_ref[...] = p3[col]

    share(2, pp_ref)
    loop(24, 64, column)

    band = jnp.where(
        lax.broadcasted_iota(jnp.int32, (64, 64), 0)
        <= lax.broadcasted_iota(jnp.int32, (64, 64), 1), rk[:, :64], 0.0,
    )
    band_ref[...] = band
    rs = -mm(lno[:, :64], lno[:, 64:], 0, 0)
    s = mm(rk[:, 64:], rs, 0, 0)

    def wait_rows(d):
        i = peer(d)
        for which in range(3):
            to = d3.at[which, core * 16 + i]
            remote(to, to, ds_sem.at[which, i], dr_sem.at[which, i], plane(i)).wait_recv()

    loop(1, 16, wait_rows)
    own = d3.at[:, mine]
    send_d = remote(own, own, one_send.at[6], one_recv.at[7], near)
    send_d.start()

    y = jnp.concatenate([panel[:WIDTH] - is_first * band, panel[WIDTH:]], axis=0)
    ys = mm(y, s)
    spread_left = jnp.concatenate([mm(y, s, 1, 1), -mm(y, rs, 1, 1)], axis=1)
    maps = jnp.concatenate([s, -rs], axis=0)

    def wait_spread(d):
        i = peer(d)
        remote(zs, zr.at[i], zs_sem.at[i], zr_sem.at[i], swap).wait_recv()
        remote(bs, br.at[i], ys_sem.at[i], yr_sem.at[i], swap).wait_recv()

    loop(1, 16, wait_spread)

    @pl.when(chip != col)
    def _():
        wait_spread(0)

    begun = mm(jnp.concatenate([from_slabs(zr, 0), from_slabs(br, 0)], axis=1), maps)
    inner = mm(ys, begun, 0, 0)

    j_ref[...] = fold(inner)
    send_j = remote(j_ref, j1_ref, one_send.at[8], one_recv.at[8], near)
    send_j.start()
    send_j.wait_recv()
    jr_ref[chip] = j_ref[half] + j1_ref[half]

    def send_inner(d):
        i = peer(d)
        remote(jr_ref.at[chip], jr_ref.at[chip], js_sem.at[i], jr_sem.at[chip], plane(i)).start()

    def wait_inner(d):
        i = peer(d)
        remote(jr_ref.at[i], jr_ref.at[i], js_sem.at[i], jr_sem.at[i], plane(i)).wait_recv()

    loop(1, 16, send_inner)

    send_d.wait_recv()
    send_d.wait_send()
    rights = []
    for which in range(3):
        rights.append(jnp.concatenate([from_slabs(d3.at[which], 0), from_slabs(d3.at[which], 16)], axis=0))
    zero_col = (col == 0).astype(F32)
    yc = jnp.concatenate([rights[2][:WIDTH] - zero_col * band, rights[2][WIDTH:]], axis=0)
    yc_ref[...] = yc
    right = jnp.concatenate([rights[0], rights[1], yc], axis=1)
    whole_left = jnp.concatenate([spread_left, begun], axis=1)
    for b in range(3):
        cut = slice(256 * b, 256 * b + 256)
        base_ref[:, cut] = a_ref[:, cut] - mm(whole_left, right[cut], 1, 1)

    loop(1, 16, wait_inner)
    total = jr_ref[0]
    for i in range(1, 16):
        total = total + jr_ref[i]
    jx_ref[half] = total
    send_jx = remote(jx_ref.at[half], jx_ref.at[half], one_send.at[9], one_recv.at[9], near)
    send_jx.start()

    send_gh.wait_send()
    send_t.wait_send()
    send_gx.wait_send()
    send_j.wait_send()

    @pl.when(chip != col)
    def _():
        send_pp.wait_send()

    @pl.when(row == 0)
    def _():
        send_b.wait_send()

    def sent(d):
        i = peer(d)
        remote(gs_ref.at[0], gr_ref.at[chip], gs_sem.at[i], gr_sem.at[chip], plane(i)).wait_send()
        remote(t3.at[i], tr.at[chip], ts_sem.at[i], tr_sem.at[chip], plane(i)).wait_send()
        remote(jr_ref.at[chip], jr_ref.at[chip], js_sem.at[i], jr_sem.at[chip], plane(i)).wait_send()
        for which in range(3):
            remote(zs, zs, ds_sem.at[which, i], dr_sem.at[which, i], plane(i)).wait_send()

    loop(1, 16, sent)

    @pl.when(chip == 0)
    def _():
        def head_sent(d):
            i = peer(d)
            remote(gs_ref.at[1], hx_ref, hs_sem.at[i], one_recv.at[5], plane(i)).wait_send()
            remote(b3.at[i], bs, bs_sem.at[i], one_recv.at[6], plane(i)).wait_send()

        loop(1, 16, head_sent)

    def spread_sent(d):
        z = (col + d) % 16
        remote(zs, zr.at[chip], zs_sem.at[z], zr_sem.at[chip], swap).wait_send()
        remote(bs, br.at[chip], ys_sem.at[z], yr_sem.at[chip], swap).wait_send()

    loop(1, 16, spread_sent)

    @pl.when(chip != col)
    def _():
        spread_sent(0)

    send_jx.wait_recv()
    yj_ref[...] = mm(y, unfold(jx_ref[...]))
    send_jx.wait_send()


def gathered(matrix, panel):
    dma = pltpu.SemaphoreType.DMA
    vmem = pltpu.VMEM
    slabs = lambda *lead: vmem((*lead, SLAB, 128), F32)
    return pl.pallas_call(
        gather_kernel,
        out_shape=(
            jax.ShapeDtypeStruct((WIDTH, WIDTH), F32),
            jax.ShapeDtypeStruct((ROWS, COLS), F32),
            jax.ShapeDtypeStruct((ROWS, WIDTH), F32),
            jax.ShapeDtypeStruct((COLS, WIDTH), F32),
        ),
        in_specs=[pl.BlockSpec(memory_space=pltpu.HBM)] * 2,
        out_specs=[pl.BlockSpec(memory_space=pltpu.VMEM)] * 4,
        scratch_shapes=[
            vmem((ROWS, COLS), F32),
            vmem((WIDTH, ROWS), F32),
            slabs(16), slabs(), slabs(32), slabs(16), slabs(16), slabs(),
            slabs(32), slabs(), slabs(3, 32), slabs(16), slabs(16),
            vmem((2, 32, 128), F32),
            vmem((2, 32, 128), F32),
            vmem((16, 16, 128), F32),
            vmem((2, 32, 128), F32),
            vmem((16, 128), F32),
            vmem((2, 16, 128), F32),
            vmem((32, 128), F32),
            vmem((32, 128), F32),
            vmem((16, 16, 128), F32),
            vmem((32, 128), F32),
        ]
        + [vmem((64, 128), F32)] * 5
        + [dma((4,)), dma((10,)), dma((10,))]
        + [dma((16,))] * 12
        + [dma((3, 16))] * 2,
        compiler_params=pltpu.CompilerParams(
            collective_id=0, has_side_effects=True, vmem_limit_bytes=40 * 1024 * 1024
        ),
        cost_estimate=pl.CostEstimate(flops=10**9, bytes_accessed=10**7, transcendentals=0),
    )(matrix, panel.T)


def update_kernel(base_ref, yj_ref, yc_ref, band_ref, out_ref, band_out):
    band_out[...] = band_ref[...]
    yj = yj_ref[...]
    for b in range(3):
        cut = slice(256 * b, 256 * b + 256)
        out_ref[:, cut] = base_ref[:, cut] + mm(yj, yc_ref[cut], 1, 1)


def body(matrix, panel):
    band, base, yj, yc = gathered(matrix, panel)
    return pl.pallas_call(
        update_kernel,
        out_shape=(
            jax.ShapeDtypeStruct((ROWS, COLS), F32),
            jax.ShapeDtypeStruct((WIDTH, WIDTH), F32),
        ),
        compiler_params=pltpu.CompilerParams(vmem_limit_bytes=40 * 1024 * 1024),
        cost_estimate=pl.CostEstimate(flops=10**8, bytes_accessed=10**7, transcendentals=0),
    )(base, yj, yc, band)


def solution(mesh):
    return jax.shard_map(
        body,
        mesh=mesh,
        in_specs=(P("row", "col"), P("row", None)),
        out_specs=(P("row", "col"), P()),
        check_vma=False,
    )
```

```python
import jax
import jax.numpy as jnp
from jax import lax
from jax.experimental import pallas as pl
from jax.experimental.pallas import tpu as pltpu
from jax.sharding import PartitionSpec as P

F32 = jnp.float32
precise = lax.Precision.HIGHEST
ROWS, COLS, WIDTH = 384, 768, 64
SLAB = 12
HALF = 192


def mm(a, b, ca=1, cb=0):
    return lax.dot_general(
        a, b, (((ca,), (cb,)), ((), ())), precision=precise, preferred_element_type=F32
    )


def halves(x):
    high = x.astype(jnp.bfloat16)
    return high, (x - high.astype(F32)).astype(jnp.bfloat16)


def mm3(a, b):
    (ah, al), (bh, bl) = a, b
    dot = lambda u, v: lax.dot_general(
        u, v, (((1,), (1,)), ((), ())), preferred_element_type=F32
    )
    return dot(ah, bh) + (dot(ah, bl) + dot(al, bh))


def loop(lo, hi, step):
    lax.fori_loop(lo, hi, lambda i, carry: (step(i), carry)[1], 0)


def fold(block):
    rows = block.shape[0] // 2
    return jnp.concatenate([block[:rows], block[rows:]], axis=1)


def unfold(block):
    return jnp.concatenate([block[:, :64], block[:, 64:]], axis=0)


def to_slabs(ref, lead, block):
    folded = fold(block)
    for i in range(16):
        ref[lead + i] = folded[SLAB * i : SLAB * i + SLAB]


def from_slabs(read):
    return unfold(jnp.concatenate([read(i) for i in range(16)], axis=0))


def gather_kernel(
    a_hbm, p_hbm, band_ref, base_ref, yj_ref, yc_ref,
    a_ref, pt_ref, p3, t3, t1, tr, own3, b3, d3, zr, br,
    gh_ref, gh1_ref, gr_ref, gx_ref, hx_ref, gs_ref,
    j_ref, j1_ref, jr_ref, jx_ref,
    gk, hh, ln, rk, lno,
    load_sem, one_send, one_recv,
    gs_sem, gr_sem, hs_sem, ts_sem, tr_sem, bs_sem,
    zs_sem, zr_sem, ys_sem, yr_sem, js_sem, jr_sem, ds_sem, dr_sem,
):
    row = lax.axis_index("row")
    col = lax.axis_index("col")
    chip = row // 2
    core = row % 2
    other = 1 - core
    near = (chip * 2 + other, col)
    swap = (col * 2 + core, chip)

    zs, bs, pp_ref = own3.at[0], own3.at[1], own3.at[2]
    loads = [pltpu.make_async_copy(p_hbm, pt_ref, load_sem.at[0])]
    for b in range(3):
        cut = pl.ds(256 * b, 256)
        loads.append(pltpu.make_async_copy(a_hbm.at[:, cut], a_ref.at[:, cut], load_sem.at[1 + b]))
    for load in loads:
        load.start()

    def peer(d):
        return (chip + d) % 16

    def plane(i):
        return (i * 2 + core, col)

    def remote(src, dst, send, recv, device):
        return pltpu.make_async_remote_copy(
            src_ref=src, dst_ref=dst, send_sem=send, recv_sem=recv,
            device_id=device, device_id_type=pl.DeviceIdType.MESH,
        )

    barrier = pltpu.get_barrier_semaphore()

    def greet(device):
        pl.semaphore_signal(
            barrier, inc=1, device_id=device, device_id_type=pl.DeviceIdType.MESH
        )

    loop(1, 16, lambda d: greet((peer(d) * 2 + core, chip)))

    @pl.when(chip != col)
    def _():
        greet((row, chip))

    loop(1, 16, lambda d: greet(plane(peer(d))))
    greet(near)

    @pl.when(chip > 0)
    def _():
        @pl.when(core == 1)
        def _():
            greet((0, col))

    loads[0].wait()
    pt = pt_ref[...]
    panel = pt.T
    is_first = (row == 0).astype(F32)
    gh_ref[0] = fold(mm(pt, pt, 1, 1))
    gh_ref[1] = fold(panel[:WIDTH]) * is_first
    to_slabs(p3, 0, panel)
    parts = []
    for b in range(3):
        loads[1 + b].wait()
        parts.append(mm(pt, a_ref[:, 256 * b : 256 * b + 256]).T)
    partial = jnp.concatenate(parts, axis=0)
    to_slabs(t3, 0, partial[:ROWS])
    to_slabs(t3, 16, partial[ROWS:])

    @pl.when(row > 0)
    def _():
        @pl.when(chip != col)
        def _():
            pl.semaphore_wait(barrier, 32)

        @pl.when(chip == col)
        def _():
            pl.semaphore_wait(barrier, 31)

    @pl.when(row == 0)
    def _():
        @pl.when(col > 0)
        def _():
            pl.semaphore_wait(barrier, 47)

        @pl.when(col == 0)
        def _():
            pl.semaphore_wait(barrier, 46)

    send_gh = remote(gh_ref, gh1_ref, one_send.at[0], one_recv.at[0], near)
    send_gh.start()
    send_t = remote(t3.at[pl.ds(other * 16, 16)], t1, one_send.at[2], one_recv.at[2], near)
    send_t.start()

    send_pp = remote(p3.at[col], pp_ref, one_send.at[1], one_recv.at[1], swap)

    @pl.when(chip != col)
    def _():
        send_pp.start()

    def first_slab(i, k):
        return remote(
            b3.at[k * 16 + i], bs, bs_sem.at[k * 16 + i], one_recv.at[6], (i * 2 + k, col)
        )

    @pl.when(row == 0)
    def _():
        first_columns = a_ref[:WIDTH].T
        to_slabs(b3, 0, first_columns[:ROWS])
        to_slabs(b3, 16, first_columns[ROWS:])
        loop(1, 16, lambda i: first_slab(i, 0).start())
        loop(0, 16, lambda i: first_slab(i, 1).start())
        bs[...] = b3[0]

    send_gh.wait_recv()
    half = pl.ds(pl.multiple_of(core * 16, 8), 16)
    gs_ref[0] = gh_ref[0, half] + gh1_ref[0, half]
    gs_ref[1] = gh_ref[1, half] + gh1_ref[1, half]

    def send_gram(d):
        i = peer(d)
        remote(gs_ref.at[0], gr_ref.at[chip], gs_sem.at[i], gr_sem.at[chip], plane(i)).start()

    def send_head(d):
        i = peer(d)
        remote(gs_ref.at[1], hx_ref, hs_sem.at[i], one_recv.at[5], plane(i)).start()

    loop(1, 16, send_gram)

    @pl.when(chip == 0)
    def _():
        loop(1, 16, send_head)

    gr_ref[chip] = gs_ref[0]

    send_t.wait_recv()
    mine = pl.ds(core * 16, 16)
    t3[mine] = t3[mine] + t1[...]

    def send_part(d):
        i = peer(d)
        remote(t3.at[core * 16 + i], tr.at[chip], ts_sem.at[i], tr_sem.at[chip], plane(i)).start()

    loop(1, 16, send_part)
    tr[chip] = t3[core * 16 + chip]

    slot = core * 16 + chip

    def spread(src, dst, send, recv):
        def step(d):
            z = (col + d) % 16
            remote(src, dst.at[chip], send.at[z], recv.at[chip], (col * 2 + core, z)).start()

        loop(1, 16, step)

        @pl.when(chip != col)
        def _():
            step(0)

        @pl.when(chip == col)
        def _():
            dst[chip] = src[...]

    @pl.when(row > 0)
    def _():
        first_slab(0, 0).wait_recv()

    spread(bs, br, ys_sem, yr_sem)

    def wait_gram(d):
        i = peer(d)
        remote(gs_ref.at[0], gr_ref.at[i], gs_sem.at[i], gr_sem.at[i], plane(i)).wait_recv()

    loop(1, 16, wait_gram)
    total = gr_ref[0]
    for i in range(1, 16):
        total = total + gr_ref[i]

    @pl.when(chip != 0)
    def _():
        remote(gs_ref.at[1], hx_ref, hs_sem.at[0], one_recv.at[5], plane(0)).wait_recv()

    @pl.when(chip == 0)
    def _():
        hx_ref[...] = gs_ref[1]

    gx_ref[0, half] = total
    gx_ref[1, half] = hx_ref[...]
    send_gx = remote(
        gx_ref.at[:, half], gx_ref.at[:, half], one_send.at[4], one_recv.at[4], near
    )
    send_gx.start()

    def wait_part(d):
        i = peer(d)
        remote(t3.at[core * 16 + i], tr.at[i], ts_sem.at[i], tr_sem.at[i], plane(i)).wait_recv()

    loop(1, 16, wait_part)
    total = tr[0]
    for i in range(1, 16):
        total = total + tr[i]
    zs[...] = total
    spread(zs, zr, zs_sem, zr_sem)

    send_gx.wait_recv()
    gram = unfold(gx_ref[0])
    head = unfold(gx_ref[1])
    eye = jnp.where(
        lax.broadcasted_iota(jnp.int32, (64, 64), 0)
        == lax.broadcasted_iota(jnp.int32, (64, 64), 1), 1.0, 0.0,
    )
    gk[...] = jnp.concatenate([gram, eye], axis=1)
    hh[...] = jnp.concatenate([head, head.T], axis=1)
    ln[...] = jnp.concatenate([eye, eye], axis=1)

    lane = lax.broadcasted_iota(jnp.int32, (64, 128), 1)
    deep = lax.broadcasted_iota(jnp.int32, (64, 128), 0)
    lane1 = lax.broadcasted_iota(jnp.int32, (1, 128), 1)
    left = lane < 64
    left1 = lane1 < 64

    def pick(x, at, j):
        return jnp.sum(jnp.where(at == j, x, 0.0), axis=1, keepdims=True)

    def inverse_root(x):
        guess = lax.rsqrt(x)
        return guess * (1.5 - 0.5 * x * guess * guess)

    def pair(step):
        j = 2 * step
        i = j + 1
        one, two = pl.ds(j, 1), pl.ds(i, 1)
        g, h, l = gk[...], hh[...], ln[...]
        g1, g2, h1, h2, l1, l2 = gk[one], gk[two], hh[one], hh[two], ln[one], ln[two]
        a, b, d = pick(g1, lane1, j), pick(g1, lane1, i), pick(g2, lane1, i)
        h11, h12 = pick(h1, lane1, j), pick(h1, lane1, i)
        h21, h22 = pick(h2, lane1, j), pick(h2, lane1, i)
        gc1, gc2 = pick(g, lane, j), pick(g, lane, i)
        hc1, hc2 = pick(h, lane, j), pick(h, lane, i)
        mc1, mc2 = pick(h, lane, j + 64), pick(h, lane, i + 64)
        inv1 = inverse_root(a)
        s1, c1, t = g1 * inv1, gc1 * inv1, b * inv1
        rest = d - t * t
        inv2 = inverse_root(rest)
        s2, c2 = (g2 - t * s1) * inv2, (gc2 - t * c1) * inv2
        rk[one] = -s1
        rk[two] = -s2
        gk[...] = g - c1 * s1 - c2 * s2
        turn1 = 1.0 / (h11 + a * inv1)
        m12 = h12 + t
        l21 = h21 * turn1
        turn2 = 1.0 / (h22 - l21 * m12 + rest * inv2)
        lc1, mr1 = hc1 * turn1, mc1 + c1
        lc2, mr2 = (hc2 - lc1 * m12) * turn2, mc2 - mr1 * l21 + c2
        f1 = jnp.where(deep > j, jnp.where(left, lc1, mr1), 0.0)
        f2 = jnp.where(deep > i, jnp.where(left, lc2, mr2), 0.0)
        f21 = jnp.where(left1, l21, m12)
        hl1 = jnp.where(left1, h1 + s1, h1 * turn1)
        h2 = h2 - f21 * hl1
        hl2 = jnp.where(left1, h2 + s2, h2 * turn2)
        ll1 = jnp.where(left1, l1, l1 * turn1)
        l2 = l2 - f21 * ll1
        ll2 = jnp.where(left1, l2, l2 * turn2)
        lno[one] = ll1
        lno[two] = ll2
        hh[...] = h - f1 * hl1 - f2 * hl2
        ln[...] = l - f1 * ll1 - f2 * ll2

    loop(0, 12, pair)

    @pl.when(chip != col)
    def _():
        send_pp.wait_recv()

    @pl.when(chip == col)
    def _():
        pp_ref[...] = p3[col]

    slot = core * 16 + chip

    def share(d):
        i = peer(d)
        return remote(own3, d3.at[slot], ds_sem.at[i], dr_sem.at[chip], plane(i))

    loop(1, 16, lambda d: share(d).start())
    d3[slot] = own3[...]
    loop(12, 32, pair)

    band = jnp.where(
        lax.broadcasted_iota(jnp.int32, (64, 64), 0)
        <= lax.broadcasted_iota(jnp.int32, (64, 64), 1), rk[:, :64], 0.0,
    )
    band_ref[...] = band
    rs = -mm(lno[:, :64], lno[:, 64:], 0, 0)
    s = mm(rk[:, 64:], rs, 0, 0)

    def wait_rows(d):
        i = peer(d)
        to = d3.at[core * 16 + i]
        remote(to, to, ds_sem.at[i], dr_sem.at[i], plane(i)).wait_recv()

    loop(1, 16, wait_rows)
    own = d3.at[mine]
    send_d = remote(own, own, one_send.at[6], one_recv.at[7], near)
    send_d.start()

    y = jnp.concatenate([panel[:WIDTH] - is_first * band, panel[WIDTH:]], axis=0)
    ys = mm(y, s)
    spread_left = jnp.concatenate([mm(y, s, 1, 1), -mm(y, rs, 1, 1)], axis=1)
    maps = jnp.concatenate([s, -rs], axis=0)

    def wait_spread(d):
        i = peer(d)
        remote(zs, zr.at[i], zs_sem.at[i], zr_sem.at[i], swap).wait_recv()
        remote(bs, br.at[i], ys_sem.at[i], yr_sem.at[i], swap).wait_recv()

    loop(1, 16, wait_spread)

    @pl.when(chip != col)
    def _():
        wait_spread(0)

    begun = mm(jnp.concatenate([from_slabs(lambda i: zr[i]), from_slabs(lambda i: br[i])], axis=1), maps)
    inner = mm(ys, begun, 0, 0)

    j_ref[...] = fold(inner)
    send_j = remote(j_ref, j1_ref, one_send.at[8], one_recv.at[8], near)
    send_j.start()
    send_j.wait_recv()
    jr_ref[chip] = j_ref[half] + j1_ref[half]

    def send_inner(d):
        i = peer(d)
        remote(jr_ref.at[chip], jr_ref.at[chip], js_sem.at[i], jr_sem.at[chip], plane(i)).start()

    def wait_inner(d):
        i = peer(d)
        remote(jr_ref.at[i], jr_ref.at[i], js_sem.at[i], jr_sem.at[i], plane(i)).wait_recv()

    loop(1, 16, send_inner)

    send_d.wait_recv()
    send_d.wait_send()
    rights = [
        jnp.concatenate(
            [from_slabs(lambda i: d3[k * 16 + i, which]) for k in range(2)], axis=0
        )
        for which in range(3)
    ]
    zero_col = (col == 0).astype(F32)
    yc = jnp.concatenate([rights[2][:WIDTH] - zero_col * band, rights[2][WIDTH:]], axis=0)
    yc_ref[...] = yc
    right = jnp.concatenate([rights[0], rights[1], yc], axis=1)
    whole_left = halves(jnp.concatenate([spread_left, begun], axis=1))
    for b in range(3):
        cut = slice(256 * b, 256 * b + 256)
        base_ref[:, cut] = a_ref[:, cut] - mm3(whole_left, halves(right[cut]))

    send_gh.wait_send()
    send_t.wait_send()
    send_gx.wait_send()
    send_j.wait_send()

    @pl.when(chip != col)
    def _():
        send_pp.wait_send()

    def sent(d):
        i = peer(d)
        remote(gs_ref.at[0], gr_ref.at[chip], gs_sem.at[i], gr_sem.at[chip], plane(i)).wait_send()
        remote(t3.at[i], tr.at[chip], ts_sem.at[i], tr_sem.at[chip], plane(i)).wait_send()
        share(d).wait_send()

    loop(1, 16, sent)

    @pl.when(chip == 0)
    def _():
        def head_sent(d):
            i = peer(d)
            remote(gs_ref.at[1], hx_ref, hs_sem.at[i], one_recv.at[5], plane(i)).wait_send()

        loop(1, 16, head_sent)

    @pl.when(row == 0)
    def _():
        loop(1, 16, lambda i: first_slab(i, 0).wait_send())
        loop(0, 16, lambda i: first_slab(i, 1).wait_send())

    def spread_sent(d):
        z = (col + d) % 16
        remote(zs, zr.at[chip], zs_sem.at[z], zr_sem.at[chip], swap).wait_send()
        remote(bs, br.at[chip], ys_sem.at[z], yr_sem.at[chip], swap).wait_send()

    loop(1, 16, spread_sent)

    @pl.when(chip != col)
    def _():
        spread_sent(0)

    loop(1, 16, wait_inner)
    total = jr_ref[0]
    for i in range(1, 16):
        total = total + jr_ref[i]
    jx_ref[half] = total
    send_jx = remote(jx_ref.at[half], jx_ref.at[half], one_send.at[9], one_recv.at[9], near)
    send_jx.start()

    def inner_sent(d):
        i = peer(d)
        remote(jr_ref.at[chip], jr_ref.at[chip], js_sem.at[i], jr_sem.at[chip], plane(i)).wait_send()

    loop(1, 16, inner_sent)
    send_jx.wait_recv()
    yj_ref[...] = mm(y, unfold(jx_ref[...]))
    send_jx.wait_send()


def gathered(matrix, panel):
    dma = pltpu.SemaphoreType.DMA
    vmem = pltpu.VMEM
    slabs = lambda *lead: vmem((*lead, SLAB, 128), F32)
    return pl.pallas_call(
        gather_kernel,
        out_shape=(
            jax.ShapeDtypeStruct((WIDTH, WIDTH), F32),
            jax.ShapeDtypeStruct((ROWS, COLS), F32),
            jax.ShapeDtypeStruct((ROWS, WIDTH), F32),
            jax.ShapeDtypeStruct((COLS, WIDTH), F32),
        ),
        in_specs=[pl.BlockSpec(memory_space=pltpu.HBM)] * 2,
        out_specs=[pl.BlockSpec(memory_space=pltpu.VMEM)] * 4,
        scratch_shapes=[
            vmem((ROWS, COLS), F32),
            vmem((WIDTH, ROWS), F32),
            slabs(16), slabs(32), slabs(16), slabs(16), slabs(3),
            slabs(32), slabs(32, 3), slabs(16), slabs(16),
            vmem((2, 32, 128), F32),
            vmem((2, 32, 128), F32),
            vmem((16, 16, 128), F32),
            vmem((2, 32, 128), F32),
            vmem((16, 128), F32),
            vmem((2, 16, 128), F32),
            vmem((32, 128), F32),
            vmem((32, 128), F32),
            vmem((16, 16, 128), F32),
            vmem((32, 128), F32),
        ]
        + [vmem((64, 128), F32)] * 5
        + [dma((4,)), dma((10,)), dma((10,))]
        + [dma((16,))] * 5
        + [dma((32,))]
        + [dma((16,))] * 8,
        compiler_params=pltpu.CompilerParams(
            collective_id=0, has_side_effects=True, vmem_limit_bytes=40 * 1024 * 1024
        ),
        cost_estimate=pl.CostEstimate(flops=10**9, bytes_accessed=10**7, transcendentals=0),
    )(matrix, panel)


def update_kernel(base_ref, yj_ref, yc_ref, band_ref, out_hbm, band_out, out, done):
    band_out[...] = band_ref[...]
    yc = halves(yc_ref[...])
    copies = []
    for b in range(3):
        cut = slice(128 * b, 128 * b + 128)
        out[cut] = base_ref[cut] + mm3(halves(yj_ref[cut]), yc)
        copies.append(pltpu.make_async_copy(out.at[cut], out_hbm.at[cut], done.at[b]))
        copies[-1].start()
    for copy in copies:
        copy.wait()


def body(matrix, panel):
    matrix = pltpu.with_memory_space_constraint(matrix, pltpu.HBM)
    panel = pltpu.with_memory_space_constraint(panel.T, pltpu.HBM)
    band, base, yj, yc = gathered(matrix, panel)
    return pl.pallas_call(
        update_kernel,
        out_shape=(
            jax.ShapeDtypeStruct((ROWS, COLS), F32),
            jax.ShapeDtypeStruct((WIDTH, WIDTH), F32),
        ),
        in_specs=[pl.BlockSpec(memory_space=pltpu.VMEM)] * 4,
        out_specs=(
            pl.BlockSpec(memory_space=pltpu.HBM),
            pl.BlockSpec(memory_space=pltpu.VMEM),
        ),
        scratch_shapes=[pltpu.VMEM((ROWS, COLS), F32), pltpu.SemaphoreType.DMA((3,))],
        compiler_params=pltpu.CompilerParams(vmem_limit_bytes=40 * 1024 * 1024),
        cost_estimate=pl.CostEstimate(flops=10**8, bytes_accessed=10**7, transcendentals=0),
    )(base, yj, yc, band)


def solution(mesh):
    return jax.shard_map(
        body,
        mesh=mesh,
        in_specs=(P("row", "col"), P("row", None)),
        out_specs=(P("row", "col"), P()),
        check_vma=False,
    )
```

```python
import jax
import jax.numpy as jnp
from jax import lax
from jax.experimental import pallas as pl
from jax.experimental.pallas import tpu as pltpu
from jax.sharding import PartitionSpec as P

F32 = jnp.float32
precise = lax.Precision.HIGHEST
ROWS, COLS, WIDTH = 384, 768, 64
SLAB = 12
HALF = 192


def mm(a, b, ca=1, cb=0):
    return lax.dot_general(
        a, b, (((ca,), (cb,)), ((), ())), precision=precise, preferred_element_type=F32
    )


def halves(x):
    high = x.astype(jnp.bfloat16)
    return high, (x - high.astype(F32)).astype(jnp.bfloat16)


def mm3(a, b):
    (ah, al), (bh, bl) = a, b
    dot = lambda u, v: lax.dot_general(
        u, v, (((1,), (1,)), ((), ())), preferred_element_type=F32
    )
    return dot(ah, bh) + (dot(ah, bl) + dot(al, bh))


def loop(lo, hi, step):
    lax.fori_loop(lo, hi, lambda i, carry: (step(i), carry)[1], 0)


def fold(block):
    rows = block.shape[0] // 2
    return jnp.concatenate([block[:rows], block[rows:]], axis=1)


def unfold(block):
    return jnp.concatenate([block[:, :64], block[:, 64:]], axis=0)


def to_slabs(ref, lead, block):
    folded = fold(block)
    for i in range(16):
        ref[lead + i] = folded[SLAB * i : SLAB * i + SLAB]


def from_slabs(read):
    return unfold(jnp.concatenate([read(i) for i in range(16)], axis=0))


def gather_kernel(
    a_hbm, p_hbm, band_ref, base_ref, yj_ref, yc_ref,
    a_ref, pt_ref, p3, t3, t1, tr, own3, b3, d3, zr, br,
    gh_ref, gh1_ref, gr_ref, gx_ref, hx_ref, gs_ref,
    j_ref, j1_ref, jr_ref, jx_ref,
    gk, hh, ln, rk, lno,
    load_sem, one_send, one_recv,
    gs_sem, gr_sem, hs_sem, ts_sem, tr_sem, bs_sem,
    zs_sem, zr_sem, ys_sem, yr_sem, js_sem, jr_sem, ds_sem, dr_sem,
):
    row = lax.axis_index("row")
    col = lax.axis_index("col")
    chip = row // 2
    core = row % 2
    other = 1 - core
    near = (chip * 2 + other, col)
    swap = (col * 2 + core, chip)

    zs, bs, pp_ref = own3.at[0], own3.at[1], own3.at[2]
    loads = [pltpu.make_async_copy(p_hbm, pt_ref, load_sem.at[0])]
    for b in range(3):
        cut = pl.ds(256 * b, 256)
        loads.append(pltpu.make_async_copy(a_hbm.at[:, cut], a_ref.at[:, cut], load_sem.at[1 + b]))
    for load in loads:
        load.start()

    def peer(d):
        return (chip + d) % 16

    def plane(i):
        return (i * 2 + core, col)

    def remote(src, dst, send, recv, device):
        return pltpu.make_async_remote_copy(
            src_ref=src, dst_ref=dst, send_sem=send, recv_sem=recv,
            device_id=device, device_id_type=pl.DeviceIdType.MESH,
        )

    barrier = pltpu.get_barrier_semaphore()

    def greet(device):
        pl.semaphore_signal(
            barrier, inc=1, device_id=device, device_id_type=pl.DeviceIdType.MESH
        )

    loop(1, 16, lambda d: greet((peer(d) * 2 + core, chip)))

    @pl.when(chip != col)
    def _():
        greet((row, chip))

    loop(1, 16, lambda d: greet(plane(peer(d))))
    greet(near)

    @pl.when(chip > 0)
    def _():
        @pl.when(core == 1)
        def _():
            greet((0, col))

    ring = (col + 8) % 16 - 8
    beside = jnp.where(ring < 0, -ring, ring)

    @pl.when(beside > 0)
    def _():
        @pl.when(beside < 3)
        def _():
            greet((row, 0))

    loads[0].wait()
    pt = pt_ref[...]
    panel = pt.T
    is_first = (row == 0).astype(F32)
    gh_ref[0] = fold(mm(pt, pt, 1, 1))
    gh_ref[1] = fold(panel[:WIDTH]) * is_first
    to_slabs(p3, 0, panel)
    parts = []
    for b in range(3):
        loads[1 + b].wait()
        parts.append(mm(pt, a_ref[:, 256 * b : 256 * b + 256]).T)
    partial = jnp.concatenate(parts, axis=0)
    to_slabs(t3, 0, partial[:ROWS])
    to_slabs(t3, 16, partial[ROWS:])

    @pl.when(col == 0)
    def _():
        to_slabs(br, 0, a_ref[:, :WIDTH])

    @pl.when(row == 0)
    def _():
        first_columns = a_ref[:WIDTH].T
        to_slabs(b3, 0, first_columns[:ROWS])
        to_slabs(b3, 16, first_columns[ROWS:])
        bs[...] = b3[0]

        @pl.when(col == 0)
        def _():
            pl.semaphore_wait(barrier, 50)

        @pl.when(col > 0)
        def _():
            pl.semaphore_wait(barrier, 47)

    @pl.when(row > 0)
    def _():
        @pl.when(col == 0)
        def _():
            @pl.when(chip == 0)
            def _():
                pl.semaphore_wait(barrier, 35)

            @pl.when(chip > 0)
            def _():
                pl.semaphore_wait(barrier, 36)

        @pl.when(col > 0)
        def _():
            @pl.when(chip == col)
            def _():
                pl.semaphore_wait(barrier, 31)

            @pl.when(chip != col)
            def _():
                pl.semaphore_wait(barrier, 32)

    send_gh = remote(gh_ref, gh1_ref, one_send.at[0], one_recv.at[0], near)
    send_gh.start()
    send_t = remote(t3.at[pl.ds(other * 16, 16)], t1, one_send.at[2], one_recv.at[2], near)
    send_t.start()

    send_pp = remote(p3.at[col], pp_ref, one_send.at[1], one_recv.at[1], swap)

    @pl.when(chip != col)
    def _():
        send_pp.start()

    def first_slab(i, k):
        return remote(
            b3.at[k * 16 + i], bs, bs_sem.at[k * 16 + i], one_recv.at[6], (i * 2 + k, col)
        )

    def first_rows_to(z):
        return remote(br, br, ys_sem.at[z], one_recv.at[10], (row, z))

    @pl.when(row == 0)
    def _():
        loop(1, 16, lambda i: first_slab(i, 0).start())
        loop(0, 16, lambda i: first_slab(i, 1).start())

    send_gh.wait_recv()
    half = pl.ds(pl.multiple_of(core * 16, 8), 16)
    gs_ref[0] = gh_ref[0, half] + gh1_ref[0, half]
    gs_ref[1] = gh_ref[1, half] + gh1_ref[1, half]

    def send_gram(d):
        i = peer(d)
        remote(gs_ref.at[0], gr_ref.at[chip], gs_sem.at[i], gr_sem.at[chip], plane(i)).start()

    def send_head(d):
        i = peer(d)
        remote(gs_ref.at[1], hx_ref, hs_sem.at[i], one_recv.at[5], plane(i)).start()

    loop(1, 16, send_gram)

    @pl.when(chip == 0)
    def _():
        loop(1, 16, send_head)

    gr_ref[chip] = gs_ref[0]

    send_t.wait_recv()
    mine = pl.ds(core * 16, 16)
    t3[mine] = t3[mine] + t1[...]

    def send_part(d):
        i = peer(d)
        remote(t3.at[core * 16 + i], tr.at[chip], ts_sem.at[i], tr_sem.at[chip], plane(i)).start()

    loop(1, 16, send_part)
    tr[chip] = t3[core * 16 + chip]

    slot = core * 16 + chip

    def spread(src, dst, send, recv):
        def step(d):
            z = (col + d) % 16
            remote(src, dst.at[chip], send.at[z], recv.at[chip], (col * 2 + core, z)).start()

        loop(1, 16, step)

        @pl.when(chip != col)
        def _():
            step(0)

        @pl.when(chip == col)
        def _():
            dst[chip] = src[...]

    def wait_gram(d):
        i = peer(d)
        remote(gs_ref.at[0], gr_ref.at[i], gs_sem.at[i], gr_sem.at[i], plane(i)).wait_recv()

    loop(1, 16, wait_gram)
    total = gr_ref[0]
    for i in range(1, 16):
        total = total + gr_ref[i]

    @pl.when(chip != 0)
    def _():
        remote(gs_ref.at[1], hx_ref, hs_sem.at[0], one_recv.at[5], plane(0)).wait_recv()

    @pl.when(chip == 0)
    def _():
        hx_ref[...] = gs_ref[1]

    gx_ref[0, half] = total
    gx_ref[1, half] = hx_ref[...]
    send_gx = remote(
        gx_ref.at[:, half], gx_ref.at[:, half], one_send.at[4], one_recv.at[4], near
    )
    send_gx.start()

    def wait_part(d):
        i = peer(d)
        remote(t3.at[core * 16 + i], tr.at[i], ts_sem.at[i], tr_sem.at[i], plane(i)).wait_recv()

    loop(1, 16, wait_part)
    total = tr[0]
    for i in range(1, 16):
        total = total + tr[i]
    zs[...] = total
    spread(zs, zr, zs_sem, zr_sem)

    @pl.when(col == 0)
    def _():
        for z in (1, 15, 2, 14):
            first_rows_to(z).start()

    @pl.when(row > 0)
    def _():
        first_slab(0, 0).wait_recv()

    def first_to(d):
        z = 3 + (col + d) % 11
        return z, remote(bs, br.at[chip], ys_sem.at[z], yr_sem.at[chip], (col * 2 + core, z))

    def send_first(d):
        z, copy = first_to(d)

        @pl.when(chip != col)
        def _():
            copy.start()

        @pl.when(chip == col)
        def _():
            @pl.when(z != col)
            def _():
                copy.start()

            @pl.when(z == col)
            def _():
                br[chip] = bs[...]

    loop(0, 11, send_first)

    send_gx.wait_recv()
    gram = unfold(gx_ref[0])
    head = unfold(gx_ref[1])
    eye = jnp.where(
        lax.broadcasted_iota(jnp.int32, (64, 64), 0)
        == lax.broadcasted_iota(jnp.int32, (64, 64), 1), 1.0, 0.0,
    )
    gk[...] = jnp.concatenate([gram, eye], axis=1)
    hh[...] = jnp.concatenate([head, head.T], axis=1)
    ln[...] = jnp.concatenate([eye, eye], axis=1)

    lane = lax.broadcasted_iota(jnp.int32, (64, 128), 1)
    deep = lax.broadcasted_iota(jnp.int32, (64, 128), 0)
    lane1 = lax.broadcasted_iota(jnp.int32, (1, 128), 1)
    left = lane < 64
    left1 = lane1 < 64

    def pick(x, at, j):
        return jnp.sum(jnp.where(at == j, x, 0.0), axis=1, keepdims=True)

    def inverse_root(x):
        guess = lax.rsqrt(x)
        return guess * (1.5 - 0.5 * x * guess * guess)

    def pair(step):
        j = 2 * step
        i = j + 1
        one, two = pl.ds(j, 1), pl.ds(i, 1)
        g, h, l = gk[...], hh[...], ln[...]
        g1, g2, h1, h2, l1, l2 = gk[one], gk[two], hh[one], hh[two], ln[one], ln[two]
        a, b, d = pick(g1, lane1, j), pick(g1, lane1, i), pick(g2, lane1, i)
        h11, h12 = pick(h1, lane1, j), pick(h1, lane1, i)
        h21, h22 = pick(h2, lane1, j), pick(h2, lane1, i)
        gc1, gc2 = pick(g, lane, j), pick(g, lane, i)
        hc1, hc2 = pick(h, lane, j), pick(h, lane, i)
        mc1, mc2 = pick(h, lane, j + 64), pick(h, lane, i + 64)
        inv1 = inverse_root(a)
        s1, c1, t = g1 * inv1, gc1 * inv1, b * inv1
        rest = d - t * t
        inv2 = inverse_root(rest)
        s2, c2 = (g2 - t * s1) * inv2, (gc2 - t * c1) * inv2
        rk[one] = -s1
        rk[two] = -s2
        gk[...] = g - c1 * s1 - c2 * s2
        turn1 = 1.0 / (h11 + a * inv1)
        m12 = h12 + t
        l21 = h21 * turn1
        turn2 = 1.0 / (h22 - l21 * m12 + rest * inv2)
        lc1, mr1 = hc1 * turn1, mc1 + c1
        lc2, mr2 = (hc2 - lc1 * m12) * turn2, mc2 - mr1 * l21 + c2
        f1 = jnp.where(deep > j, jnp.where(left, lc1, mr1), 0.0)
        f2 = jnp.where(deep > i, jnp.where(left, lc2, mr2), 0.0)
        f21 = jnp.where(left1, l21, m12)
        hl1 = jnp.where(left1, h1 + s1, h1 * turn1)
        h2 = h2 - f21 * hl1
        hl2 = jnp.where(left1, h2 + s2, h2 * turn2)
        ll1 = jnp.where(left1, l1, l1 * turn1)
        l2 = l2 - f21 * ll1
        ll2 = jnp.where(left1, l2, l2 * turn2)
        lno[one] = ll1
        lno[two] = ll2
        hh[...] = h - f1 * hl1 - f2 * hl2
        ln[...] = l - f1 * ll1 - f2 * ll2

    loop(0, 12, pair)

    @pl.when(chip != col)
    def _():
        send_pp.wait_recv()

    @pl.when(chip == col)
    def _():
        pp_ref[...] = p3[col]

    slot = core * 16 + chip

    def share(d):
        i = peer(d)
        return remote(own3, d3.at[slot], ds_sem.at[i], dr_sem.at[chip], plane(i))

    loop(1, 16, lambda d: share(d).start())
    d3[slot] = own3[...]
    loop(12, 32, pair)

    band = jnp.where(
        lax.broadcasted_iota(jnp.int32, (64, 64), 0)
        <= lax.broadcasted_iota(jnp.int32, (64, 64), 1), rk[:, :64], 0.0,
    )
    band_ref[...] = band
    rs = -mm(lno[:, :64], lno[:, 64:], 0, 0)
    s = mm(rk[:, 64:], rs, 0, 0)

    def wait_rows(d):
        i = peer(d)
        to = d3.at[core * 16 + i]
        remote(to, to, ds_sem.at[i], dr_sem.at[i], plane(i)).wait_recv()

    loop(1, 16, wait_rows)
    own = d3.at[mine]
    send_d = remote(own, own, one_send.at[6], one_recv.at[7], near)
    send_d.start()

    y = jnp.concatenate([panel[:WIDTH] - is_first * band, panel[WIDTH:]], axis=0)
    ys = mm(y, s)
    spread_left = jnp.concatenate([mm(y, s, 1, 1), -mm(y, rs, 1, 1)], axis=1)
    folded_ys = fold(ys)

    def twice(block):
        none = jnp.zeros_like(block)
        return jnp.concatenate(
            [jnp.concatenate([block, none], axis=1), jnp.concatenate([none, block], axis=1)],
            axis=0,
        )

    def stacked(ref):
        return jnp.concatenate([ref[i] for i in range(16)], axis=0)

    twice_s = twice(s)

    @pl.when(beside > 0)
    def _():
        @pl.when(beside < 3)
        def _():
            first_rows_to(0).wait_recv()

    @pl.when(beside > 2)
    def _():
        def wait_first(d):
            i = peer(d)
            remote(bs, br.at[i], ys_sem.at[i], yr_sem.at[i], swap).wait_recv()

        loop(1, 16, wait_first)

        @pl.when(chip != col)
        def _():
            wait_first(0)

    first_part = mm(stacked(br), twice(rs))

    def wait_spread(d):
        i = peer(d)
        remote(zs, zr.at[i], zs_sem.at[i], zr_sem.at[i], swap).wait_recv()

    loop(1, 16, wait_spread)

    @pl.when(chip != col)
    def _():
        wait_spread(0)

    folded_begun = mm(stacked(zr), twice_s) - first_part
    inner = mm(folded_ys, folded_begun, 0, 0)
    inner = inner[:64, :64] + inner[64:, 64:]

    j_ref[...] = fold(inner)
    send_j = remote(j_ref, j1_ref, one_send.at[8], one_recv.at[8], near)
    send_j.start()
    send_j.wait_recv()
    jr_ref[chip] = j_ref[half] + j1_ref[half]

    def send_inner(d):
        i = peer(d)
        remote(jr_ref.at[chip], jr_ref.at[chip], js_sem.at[i], jr_sem.at[chip], plane(i)).start()

    def wait_inner(d):
        i = peer(d)
        remote(jr_ref.at[i], jr_ref.at[i], js_sem.at[i], jr_sem.at[i], plane(i)).wait_recv()

    loop(1, 16, send_inner)

    send_d.wait_recv()
    send_d.wait_send()
    rights = [
        jnp.concatenate(
            [from_slabs(lambda i: d3[k * 16 + i, which]) for k in range(2)], axis=0
        )
        for which in range(3)
    ]
    zero_col = (col == 0).astype(F32)
    yc = jnp.concatenate([rights[2][:WIDTH] - zero_col * band, rights[2][WIDTH:]], axis=0)
    yc_ref[...] = yc
    right = jnp.concatenate([rights[0], rights[1], yc], axis=1)
    begun = unfold(folded_begun)
    whole_left = halves(jnp.concatenate([spread_left, begun], axis=1))
    for b in range(3):
        cut = slice(256 * b, 256 * b + 256)
        base_ref[:, cut] = a_ref[:, cut] - mm3(whole_left, halves(right[cut]))

    send_gh.wait_send()
    send_t.wait_send()
    send_gx.wait_send()
    send_j.wait_send()

    @pl.when(chip != col)
    def _():
        send_pp.wait_send()

    def sent(d):
        i = peer(d)
        remote(gs_ref.at[0], gr_ref.at[chip], gs_sem.at[i], gr_sem.at[chip], plane(i)).wait_send()
        remote(t3.at[i], tr.at[chip], ts_sem.at[i], tr_sem.at[chip], plane(i)).wait_send()
        share(d).wait_send()

    loop(1, 16, sent)

    @pl.when(chip == 0)
    def _():
        def head_sent(d):
            i = peer(d)
            remote(gs_ref.at[1], hx_ref, hs_sem.at[i], one_recv.at[5], plane(i)).wait_send()

        loop(1, 16, head_sent)

    @pl.when(row == 0)
    def _():
        loop(1, 16, lambda i: first_slab(i, 0).wait_send())
        loop(0, 16, lambda i: first_slab(i, 1).wait_send())

    @pl.when(col == 0)
    def _():
        for z in (1, 15, 2, 14):
            first_rows_to(z).wait_send()

    def first_sent(d):
        z, copy = first_to(d)

        @pl.when(chip != col)
        def _():
            copy.wait_send()

        @pl.when(chip == col)
        def _():
            @pl.when(z != col)
            def _():
                copy.wait_send()

    loop(0, 11, first_sent)

    def spread_sent(d):
        z = (col + d) % 16
        remote(zs, zr.at[chip], zs_sem.at[z], zr_sem.at[chip], swap).wait_send()

    loop(1, 16, spread_sent)

    @pl.when(chip != col)
    def _():
        spread_sent(0)

    loop(1, 16, wait_inner)
    total = jr_ref[0]
    for i in range(1, 16):
        total = total + jr_ref[i]
    jx_ref[half] = total
    send_jx = remote(jx_ref.at[half], jx_ref.at[half], one_send.at[9], one_recv.at[9], near)
    send_jx.start()

    def inner_sent(d):
        i = peer(d)
        remote(jr_ref.at[chip], jr_ref.at[chip], js_sem.at[i], jr_sem.at[chip], plane(i)).wait_send()

    loop(1, 16, inner_sent)
    send_jx.wait_recv()
    yj_ref[...] = mm(y, unfold(jx_ref[...]))
    send_jx.wait_send()


def gathered(matrix, panel):
    dma = pltpu.SemaphoreType.DMA
    vmem = pltpu.VMEM
    slabs = lambda *lead: vmem((*lead, SLAB, 128), F32)
    return pl.pallas_call(
        gather_kernel,
        out_shape=(
            jax.ShapeDtypeStruct((WIDTH, WIDTH), F32),
            jax.ShapeDtypeStruct((ROWS, COLS), F32),
            jax.ShapeDtypeStruct((ROWS, WIDTH), F32),
            jax.ShapeDtypeStruct((COLS, WIDTH), F32),
        ),
        in_specs=[pl.BlockSpec(memory_space=pltpu.HBM)] * 2,
        out_specs=[pl.BlockSpec(memory_space=pltpu.VMEM)] * 4,
        scratch_shapes=[
            vmem((ROWS, COLS), F32),
            vmem((WIDTH, ROWS), F32),
            slabs(16), slabs(32), slabs(16), slabs(16), slabs(3),
            slabs(32), slabs(32, 3), slabs(16), slabs(16),
            vmem((2, 32, 128), F32),
            vmem((2, 32, 128), F32),
            vmem((16, 16, 128), F32),
            vmem((2, 32, 128), F32),
            vmem((16, 128), F32),
            vmem((2, 16, 128), F32),
            vmem((32, 128), F32),
            vmem((32, 128), F32),
            vmem((16, 16, 128), F32),
            vmem((32, 128), F32),
        ]
        + [vmem((64, 128), F32)] * 5
        + [dma((4,)), dma((10,)), dma((11,))]
        + [dma((16,))] * 5
        + [dma((32,))]
        + [dma((16,))] * 8,
        compiler_params=pltpu.CompilerParams(
            collective_id=0, has_side_effects=True, vmem_limit_bytes=40 * 1024 * 1024
        ),
        cost_estimate=pl.CostEstimate(flops=10**9, bytes_accessed=10**7, transcendentals=0),
    )(matrix, panel)


def update_kernel(base_ref, yj_ref, yc_ref, band_ref, out_hbm, band_out, out, done):
    band_out[...] = band_ref[...]
    yc = halves(yc_ref[...])
    copies = []
    for b in range(3):
        cut = slice(128 * b, 128 * b + 128)
        out[cut] = base_ref[cut] + mm3(halves(yj_ref[cut]), yc)
        copies.append(pltpu.make_async_copy(out.at[cut], out_hbm.at[cut], done.at[b]))
        copies[-1].start()
    for copy in copies:
        copy.wait()


def body(matrix, panel):
    matrix = pltpu.with_memory_space_constraint(matrix, pltpu.HBM)
    panel = pltpu.with_memory_space_constraint(panel.T, pltpu.HBM)
    band, base, yj, yc = gathered(matrix, panel)
    return pl.pallas_call(
        update_kernel,
        out_shape=(
            jax.ShapeDtypeStruct((ROWS, COLS), F32),
            jax.ShapeDtypeStruct((WIDTH, WIDTH), F32),
        ),
        in_specs=[pl.BlockSpec(memory_space=pltpu.VMEM)] * 4,
        out_specs=(
            pl.BlockSpec(memory_space=pltpu.HBM),
            pl.BlockSpec(memory_space=pltpu.VMEM),
        ),
        scratch_shapes=[pltpu.VMEM((ROWS, COLS), F32), pltpu.SemaphoreType.DMA((3,))],
        compiler_params=pltpu.CompilerParams(vmem_limit_bytes=40 * 1024 * 1024),
        cost_estimate=pl.CostEstimate(flops=10**8, bytes_accessed=10**7, transcendentals=0),
    )(base, yj, yc, band)


def solution(mesh):
    return jax.shard_map(
        body,
        mesh=mesh,
        in_specs=(P("row", "col"), P("row", None)),
        out_specs=(P("row", "col"), P()),
        check_vma=False,
    )
```

```python
import jax
import jax.numpy as jnp
from jax import lax
from jax.experimental import pallas as pl
from jax.experimental.pallas import tpu as pltpu
from jax.sharding import PartitionSpec as P

F32 = jnp.float32
precise = lax.Precision.HIGHEST
ROWS, COLS, WIDTH = 384, 768, 64
SLAB = 12
HALF = 192


def mm(a, b, ca=1, cb=0):
    return lax.dot_general(
        a, b, (((ca,), (cb,)), ((), ())), precision=precise, preferred_element_type=F32
    )


def halves(x):
    high = x.astype(jnp.bfloat16)
    return high, (x - high.astype(F32)).astype(jnp.bfloat16)


def mm3(a, b):
    (ah, al), (bh, bl) = a, b
    dot = lambda u, v: lax.dot_general(
        u, v, (((1,), (1,)), ((), ())), preferred_element_type=F32
    )
    return dot(ah, bh) + (dot(ah, bl) + dot(al, bh))


def loop(lo, hi, step):
    lax.fori_loop(lo, hi, lambda i, carry: (step(i), carry)[1], 0)


def fold(block):
    rows = block.shape[0] // 2
    return jnp.concatenate([block[:rows], block[rows:]], axis=1)


def unfold(block):
    return jnp.concatenate([block[:, :64], block[:, 64:]], axis=0)


def to_slabs(ref, lead, block):
    folded = fold(block)
    for i in range(16):
        ref[lead + i] = folded[SLAB * i : SLAB * i + SLAB]


def from_slabs(read):
    return unfold(jnp.concatenate([read(i) for i in range(16)], axis=0))


def gather_kernel(
    a_hbm, p_hbm, band_ref, base_ref, yj_ref, yc_ref,
    a_ref, pt_ref, p3, t3, t1, tr, own3, b3, d3, zr, br,
    gh_ref, gh1_ref, gr_ref, gx_ref, hx_ref, gs_ref,
    j_ref, j1_ref, jr_ref,
    gk, hh, ln, rk, lno,
    load_sem, one_send, one_recv,
    gs_sem, gr_sem, hs_sem, ts_sem, tr_sem, bs_sem,
    zs_sem, zr_sem, ys_sem, yr_sem, js_sem, jr_sem, ds_sem, dr_sem,
):
    row = lax.axis_index("row")
    col = lax.axis_index("col")
    chip = row // 2
    core = row % 2
    other = 1 - core
    near = (chip * 2 + other, col)
    swap = (col * 2 + core, chip)

    zs, bs, pp_ref = own3.at[0], own3.at[1], own3.at[2]
    loads = [pltpu.make_async_copy(p_hbm, pt_ref, load_sem.at[0])]
    for b in range(3):
        cut = pl.ds(256 * b, 256)
        loads.append(pltpu.make_async_copy(a_hbm.at[:, cut], a_ref.at[:, cut], load_sem.at[1 + b]))
    for load in loads:
        load.start()

    def peer(d):
        return (chip + d) % 16

    def plane(i):
        return (i * 2 + core, col)

    def remote(src, dst, send, recv, device):
        return pltpu.make_async_remote_copy(
            src_ref=src, dst_ref=dst, send_sem=send, recv_sem=recv,
            device_id=device, device_id_type=pl.DeviceIdType.MESH,
        )

    barrier = pltpu.get_barrier_semaphore()

    def greet(device):
        pl.semaphore_signal(
            barrier, inc=1, device_id=device, device_id_type=pl.DeviceIdType.MESH
        )

    loop(1, 16, lambda d: greet((peer(d) * 2 + core, chip)))

    @pl.when(chip != col)
    def _():
        greet((row, chip))

    loop(1, 16, lambda d: greet(plane(peer(d))))
    greet(near)

    @pl.when(chip > 0)
    def _():
        @pl.when(core == 1)
        def _():
            greet((0, col))

    ring = (col + 8) % 16 - 8
    beside = jnp.where(ring < 0, -ring, ring)

    @pl.when(beside > 0)
    def _():
        @pl.when(beside < 4)
        def _():
            greet((row, 0))

    loads[0].wait()
    pt = pt_ref[...]
    panel = pt.T
    is_first = (row == 0).astype(F32)
    gh_ref[0] = fold(mm(pt, pt, 1, 1))
    gh_ref[1] = fold(panel[:WIDTH]) * is_first
    to_slabs(p3, 0, panel)
    parts = []
    for b in range(3):
        loads[1 + b].wait()
        parts.append(mm(pt, a_ref[:, 256 * b : 256 * b + 256]).T)
    partial = jnp.concatenate(parts, axis=0)
    to_slabs(t3, 0, partial[:ROWS])
    to_slabs(t3, 16, partial[ROWS:])

    @pl.when(col == 0)
    def _():
        to_slabs(br, 0, a_ref[:, :WIDTH])

    @pl.when(row == 0)
    def _():
        first_columns = a_ref[:WIDTH].T
        to_slabs(b3, 0, first_columns[:ROWS])
        to_slabs(b3, 16, first_columns[ROWS:])
        bs[...] = b3[0]

        @pl.when(col == 0)
        def _():
            pl.semaphore_wait(barrier, 52)

        @pl.when(col > 0)
        def _():
            pl.semaphore_wait(barrier, 47)

    @pl.when(row > 0)
    def _():
        @pl.when(col == 0)
        def _():
            @pl.when(chip == 0)
            def _():
                pl.semaphore_wait(barrier, 37)

            @pl.when(chip > 0)
            def _():
                pl.semaphore_wait(barrier, 38)

        @pl.when(col > 0)
        def _():
            @pl.when(chip == col)
            def _():
                pl.semaphore_wait(barrier, 31)

            @pl.when(chip != col)
            def _():
                pl.semaphore_wait(barrier, 32)

    send_t = remote(t3.at[pl.ds(other * 16, 16)], t1, one_send.at[2], one_recv.at[2], near)
    send_t.start()
    send_gh = remote(gh_ref, gh1_ref, one_send.at[0], one_recv.at[0], near)
    send_gh.start()

    send_pp = remote(p3.at[col], pp_ref, one_send.at[1], one_recv.at[1], swap)

    @pl.when(chip != col)
    def _():
        send_pp.start()

    def first_slab(i, k):
        return remote(
            b3.at[k * 16 + i], bs, bs_sem.at[k * 16 + i], one_recv.at[6], (i * 2 + k, col)
        )

    def first_rows_to(z):
        return remote(br, br, ys_sem.at[z], one_recv.at[10], (row, z))


    send_t.wait_recv()
    mine = pl.ds(core * 16, 16)
    t3[mine] = t3[mine] + t1[...]

    def send_part(d):
        i = peer(d)
        remote(t3.at[core * 16 + i], tr.at[chip], ts_sem.at[i], tr_sem.at[chip], plane(i)).start()

    loop(1, 16, send_part)
    tr[chip] = t3[core * 16 + chip]

    send_gh.wait_recv()
    half = pl.ds(pl.multiple_of(core * 16, 8), 16)
    gs_ref[0] = gh_ref[0, half] + gh1_ref[0, half]
    gs_ref[1] = gh_ref[1, half] + gh1_ref[1, half]

    def send_gram(d):
        i = peer(d)
        remote(gs_ref.at[0], gr_ref.at[chip], gs_sem.at[i], gr_sem.at[chip], plane(i)).start()

    def send_head(d):
        i = peer(d)
        remote(gs_ref.at[1], hx_ref, hs_sem.at[i], one_recv.at[5], plane(i)).start()

    loop(1, 16, send_gram)


    gr_ref[chip] = gs_ref[0]


    @pl.when(chip == 0)
    def _():
        loop(1, 16, send_head)

    @pl.when(row == 0)
    def _():
        loop(1, 16, lambda i: first_slab(i, 0).start())
        loop(0, 16, lambda i: first_slab(i, 1).start())

    slot = core * 16 + chip

    def spread(src, dst, send, recv):
        def step(d):
            z = (col + d) % 16
            remote(src, dst.at[chip], send.at[z], recv.at[chip], (col * 2 + core, z)).start()

        loop(1, 16, step)

        @pl.when(chip != col)
        def _():
            step(0)

        @pl.when(chip == col)
        def _():
            dst[chip] = src[...]

    def wait_part(d):
        i = peer(d)
        remote(t3.at[core * 16 + i], tr.at[i], ts_sem.at[i], tr_sem.at[i], plane(i)).wait_recv()

    loop(1, 16, wait_part)
    total = tr[0]
    for i in range(1, 16):
        total = total + tr[i]
    zs[...] = total
    spread(zs, zr, zs_sem, zr_sem)

    def wait_gram(d):
        i = peer(d)
        remote(gs_ref.at[0], gr_ref.at[i], gs_sem.at[i], gr_sem.at[i], plane(i)).wait_recv()

    loop(1, 16, wait_gram)
    total = gr_ref[0]
    for i in range(1, 16):
        total = total + gr_ref[i]

    @pl.when(chip != 0)
    def _():
        remote(gs_ref.at[1], hx_ref, hs_sem.at[0], one_recv.at[5], plane(0)).wait_recv()

    @pl.when(chip == 0)
    def _():
        hx_ref[...] = gs_ref[1]

    gx_ref[0, half] = total
    gx_ref[1, half] = hx_ref[...]
    send_gx = remote(
        gx_ref.at[:, half], gx_ref.at[:, half], one_send.at[4], one_recv.at[4], near
    )
    send_gx.start()


    @pl.when(col == 0)
    def _():
        for z in (1, 15, 2, 14, 3, 13):
            first_rows_to(z).start()

    @pl.when(row > 0)
    def _():
        first_slab(0, 0).wait_recv()

    def first_to(d):
        z = 4 + (col + d) % 9
        return z, remote(bs, br.at[chip], ys_sem.at[z], yr_sem.at[chip], (col * 2 + core, z))

    def send_first(d):
        z, copy = first_to(d)

        @pl.when(chip != col)
        def _():
            copy.start()

        @pl.when(chip == col)
        def _():
            @pl.when(z != col)
            def _():
                copy.start()

            @pl.when(z == col)
            def _():
                br[chip] = bs[...]

    loop(0, 9, send_first)

    send_gx.wait_recv()
    gram = unfold(gx_ref[0])
    head = unfold(gx_ref[1])
    eye = jnp.where(
        lax.broadcasted_iota(jnp.int32, (64, 64), 0)
        == lax.broadcasted_iota(jnp.int32, (64, 64), 1), 1.0, 0.0,
    )
    gk[...] = jnp.concatenate([gram, eye], axis=1)
    hh[...] = jnp.concatenate([head, head.T], axis=1)
    ln[...] = jnp.concatenate([eye, eye], axis=1)

    lane = lax.broadcasted_iota(jnp.int32, (64, 128), 1)
    deep = lax.broadcasted_iota(jnp.int32, (64, 128), 0)
    lane1 = lax.broadcasted_iota(jnp.int32, (1, 128), 1)
    left = lane < 64
    left1 = lane1 < 64

    def pick(x, at, j):
        return jnp.sum(jnp.where(at == j, x, 0.0), axis=1, keepdims=True)

    def inverse_root(x):
        guess = lax.rsqrt(x)
        return guess * (1.5 - 0.5 * x * guess * guess)

    def pair(step):
        j = 2 * step
        i = j + 1
        one, two = pl.ds(j, 1), pl.ds(i, 1)
        g, h, l = gk[...], hh[...], ln[...]
        g1, g2, h1, h2, l1, l2 = gk[one], gk[two], hh[one], hh[two], ln[one], ln[two]
        a, b, d = pick(g1, lane1, j), pick(g1, lane1, i), pick(g2, lane1, i)
        h11, h12 = pick(h1, lane1, j), pick(h1, lane1, i)
        h21, h22 = pick(h2, lane1, j), pick(h2, lane1, i)
        gc1, gc2 = pick(g, lane, j), pick(g, lane, i)
        hc1, hc2 = pick(h, lane, j), pick(h, lane, i)
        mc1, mc2 = pick(h, lane, j + 64), pick(h, lane, i + 64)
        inv1 = inverse_root(a)
        s1, c1, t = g1 * inv1, gc1 * inv1, b * inv1
        rest = d - t * t
        inv2 = inverse_root(rest)
        s2, c2 = (g2 - t * s1) * inv2, (gc2 - t * c1) * inv2
        rk[one] = -s1
        rk[two] = -s2
        gk[...] = g - c1 * s1 - c2 * s2
        turn1 = 1.0 / (h11 + a * inv1)
        m12 = h12 + t
        l21 = h21 * turn1
        turn2 = 1.0 / (h22 - l21 * m12 + rest * inv2)
        lc1, mr1 = hc1 * turn1, mc1 + c1
        lc2, mr2 = (hc2 - lc1 * m12) * turn2, mc2 - mr1 * l21 + c2
        f1 = jnp.where(deep > j, jnp.where(left, lc1, mr1), 0.0)
        f2 = jnp.where(deep > i, jnp.where(left, lc2, mr2), 0.0)
        f21 = jnp.where(left1, l21, m12)
        hl1 = jnp.where(left1, h1 + s1, h1 * turn1)
        h2 = h2 - f21 * hl1
        hl2 = jnp.where(left1, h2 + s2, h2 * turn2)
        ll1 = jnp.where(left1, l1, l1 * turn1)
        l2 = l2 - f21 * ll1
        ll2 = jnp.where(left1, l2, l2 * turn2)
        lno[one] = ll1
        lno[two] = ll2
        hh[...] = h - f1 * hl1 - f2 * hl2
        ln[...] = l - f1 * ll1 - f2 * ll2

    loop(0, 12, pair)

    @pl.when(chip != col)
    def _():
        send_pp.wait_recv()

    @pl.when(chip == col)
    def _():
        pp_ref[...] = p3[col]

    slot = core * 16 + chip

    def share(d):
        i = peer(d)
        return remote(own3, d3.at[slot], ds_sem.at[i], dr_sem.at[chip], plane(i))

    loop(1, 16, lambda d: share(d).start())
    d3[slot] = own3[...]
    loop(12, 32, pair)

    band = jnp.where(
        lax.broadcasted_iota(jnp.int32, (64, 64), 0)
        <= lax.broadcasted_iota(jnp.int32, (64, 64), 1), rk[:, :64], 0.0,
    )
    band_ref[...] = band
    rs = -mm(lno[:, :64], lno[:, 64:], 0, 0)
    s = mm(rk[:, 64:], rs, 0, 0)

    def wait_rows(d):
        i = peer(d)
        to = d3.at[core * 16 + i]
        remote(to, to, ds_sem.at[i], dr_sem.at[i], plane(i)).wait_recv()

    loop(1, 16, wait_rows)
    own = d3.at[mine]
    send_d = remote(own, own, one_send.at[6], one_recv.at[7], near)
    send_d.start()

    y = jnp.concatenate([panel[:WIDTH] - is_first * band, panel[WIDTH:]], axis=0)
    ys = mm(y, s)
    spread_left = jnp.concatenate([mm(y, s, 1, 1), -mm(y, rs, 1, 1)], axis=1)
    folded_ys = fold(ys)

    def twice(block):
        none = jnp.zeros_like(block)
        return jnp.concatenate(
            [jnp.concatenate([block, none], axis=1), jnp.concatenate([none, block], axis=1)],
            axis=0,
        )

    def stacked(ref):
        return jnp.concatenate([ref[i] for i in range(16)], axis=0)

    twice_s = twice(s)

    @pl.when(beside > 0)
    def _():
        @pl.when(beside < 4)
        def _():
            first_rows_to(0).wait_recv()

    @pl.when(beside > 3)
    def _():
        def wait_first(d):
            i = peer(d)
            remote(bs, br.at[i], ys_sem.at[i], yr_sem.at[i], swap).wait_recv()

        loop(1, 16, wait_first)

        @pl.when(chip != col)
        def _():
            wait_first(0)

    first_part = mm(stacked(br), twice(rs))

    def wait_spread(d):
        i = peer(d)
        remote(zs, zr.at[i], zs_sem.at[i], zr_sem.at[i], swap).wait_recv()

    loop(1, 16, wait_spread)

    @pl.when(chip != col)
    def _():
        wait_spread(0)

    folded_begun = mm(stacked(zr), twice_s) - first_part
    inner = mm(folded_ys, folded_begun, 0, 0)
    inner = inner[:64, :64] + inner[64:, 64:]

    at_row = lax.broadcasted_iota(jnp.int32, (32, 32), 0)
    at_lane = lax.broadcasted_iota(jnp.int32, (32, 32), 1)
    inner = 0.5 * (inner + inner.T)
    corner = inner[32:, 32:]
    mixed = jnp.where(at_row <= at_lane, inner[:32, :32], corner)
    j_ref[:16] = fold(jnp.concatenate([mixed, inner[:32, 32:]], axis=1))
    j_ref[16:, :32] = jnp.sum(jnp.where(at_row == at_lane, corner, 0.0), axis=0, keepdims=True)
    j_ref[16:, 32:] = jnp.zeros((1, 96), F32)
    send_j = remote(j_ref, j1_ref, one_send.at[8], one_recv.at[8], near)
    send_j.start()
    send_j.wait_recv()
    jr_ref[chip] = j_ref[...] + j1_ref[...]

    def send_inner(d):
        i = peer(d)
        remote(jr_ref.at[chip], jr_ref.at[chip], js_sem.at[i], jr_sem.at[chip], plane(i)).start()

    def wait_inner(d):
        i = peer(d)
        remote(jr_ref.at[i], jr_ref.at[i], js_sem.at[i], jr_sem.at[i], plane(i)).wait_recv()

    loop(1, 16, send_inner)

    send_d.wait_recv()
    send_d.wait_send()
    rights = [
        jnp.concatenate(
            [from_slabs(lambda i: d3[k * 16 + i, which]) for k in range(2)], axis=0
        )
        for which in range(3)
    ]
    zero_col = (col == 0).astype(F32)
    yc = jnp.concatenate([rights[2][:WIDTH] - zero_col * band, rights[2][WIDTH:]], axis=0)
    yc_ref[...] = yc
    right = jnp.concatenate([rights[0], rights[1], yc], axis=1)
    begun = unfold(folded_begun)
    whole_left = halves(jnp.concatenate([spread_left, begun], axis=1))
    for b in range(3):
        cut = slice(256 * b, 256 * b + 256)
        base_ref[:, cut] = a_ref[:, cut] - mm3(whole_left, halves(right[cut]))

    send_gh.wait_send()
    send_t.wait_send()
    send_gx.wait_send()
    send_j.wait_send()

    @pl.when(chip != col)
    def _():
        send_pp.wait_send()

    def sent(d):
        i = peer(d)
        remote(gs_ref.at[0], gr_ref.at[chip], gs_sem.at[i], gr_sem.at[chip], plane(i)).wait_send()
        remote(t3.at[i], tr.at[chip], ts_sem.at[i], tr_sem.at[chip], plane(i)).wait_send()
        share(d).wait_send()

    loop(1, 16, sent)

    @pl.when(chip == 0)
    def _():
        def head_sent(d):
            i = peer(d)
            remote(gs_ref.at[1], hx_ref, hs_sem.at[i], one_recv.at[5], plane(i)).wait_send()

        loop(1, 16, head_sent)

    @pl.when(row == 0)
    def _():
        loop(1, 16, lambda i: first_slab(i, 0).wait_send())
        loop(0, 16, lambda i: first_slab(i, 1).wait_send())

    @pl.when(col == 0)
    def _():
        for z in (1, 15, 2, 14, 3, 13):
            first_rows_to(z).wait_send()

    def first_sent(d):
        z, copy = first_to(d)

        @pl.when(chip != col)
        def _():
            copy.wait_send()

        @pl.when(chip == col)
        def _():
            @pl.when(z != col)
            def _():
                copy.wait_send()

    loop(0, 9, first_sent)

    def spread_sent(d):
        z = (col + d) % 16
        remote(zs, zr.at[chip], zs_sem.at[z], zr_sem.at[chip], swap).wait_send()

    loop(1, 16, spread_sent)

    @pl.when(chip != col)
    def _():
        spread_sent(0)

    loop(1, 16, wait_inner)
    total = jr_ref[0]
    for i in range(1, 16):
        total = total + jr_ref[i]
    def inner_sent(d):
        i = peer(d)
        remote(jr_ref.at[chip], jr_ref.at[chip], js_sem.at[i], jr_sem.at[chip], plane(i)).wait_send()

    loop(1, 16, inner_sent)
    packed = unfold(total[:16])
    mixed, side = packed[:, :32], packed[:, 32:]
    upper = jnp.where(at_row <= at_lane, mixed, 0.0)
    lower = jnp.where(at_row > at_lane, mixed, 0.0)
    strict = jnp.where(at_row < at_lane, mixed, 0.0)
    corner = lower + lower.T + jnp.where(at_row == at_lane, total[16:, :32], 0.0)
    coupling = jnp.concatenate(
        [
            jnp.concatenate([upper + strict.T, side], axis=1),
            jnp.concatenate([side.T, corner], axis=1),
        ],
        axis=0,
    )
    yj_ref[...] = mm(y, coupling)


def gathered(matrix, panel):
    dma = pltpu.SemaphoreType.DMA
    vmem = pltpu.VMEM
    slabs = lambda *lead: vmem((*lead, SLAB, 128), F32)
    return pl.pallas_call(
        gather_kernel,
        out_shape=(
            jax.ShapeDtypeStruct((WIDTH, WIDTH), F32),
            jax.ShapeDtypeStruct((ROWS, COLS), F32),
            jax.ShapeDtypeStruct((ROWS, WIDTH), F32),
            jax.ShapeDtypeStruct((COLS, WIDTH), F32),
        ),
        in_specs=[pl.BlockSpec(memory_space=pltpu.HBM)] * 2,
        out_specs=[pl.BlockSpec(memory_space=pltpu.VMEM)] * 4,
        scratch_shapes=[
            vmem((ROWS, COLS), F32),
            vmem((WIDTH, ROWS), F32),
            slabs(16), slabs(32), slabs(16), slabs(16), slabs(3),
            slabs(32), slabs(32, 3), slabs(16), slabs(16),
            vmem((2, 32, 128), F32),
            vmem((2, 32, 128), F32),
            vmem((16, 16, 128), F32),
            vmem((2, 32, 128), F32),
            vmem((16, 128), F32),
            vmem((2, 16, 128), F32),
            vmem((17, 128), F32),
            vmem((17, 128), F32),
            vmem((16, 17, 128), F32),
        ]
        + [vmem((64, 128), F32)] * 5
        + [dma((4,)), dma((10,)), dma((11,))]
        + [dma((16,))] * 5
        + [dma((32,))]
        + [dma((16,))] * 8,
        compiler_params=pltpu.CompilerParams(
            collective_id=0, has_side_effects=True, vmem_limit_bytes=40 * 1024 * 1024
        ),
        cost_estimate=pl.CostEstimate(flops=10**9, bytes_accessed=10**7, transcendentals=0),
    )(matrix, panel)


def update_kernel(base_ref, yj_ref, yc_ref, band_ref, out_hbm, band_out, out, done):
    band_out[...] = band_ref[...]
    yj = halves(yj_ref[...])
    copies = []
    for b in range(3):
        cut = pl.ds(256 * b, 256)
        out[:, cut] = base_ref[:, cut] + mm3(yj, halves(yc_ref[cut]))
        copies.append(pltpu.make_async_copy(out.at[:, cut], out_hbm.at[:, cut], done.at[b]))
        copies[-1].start()
    for copy in copies:
        copy.wait()


def body(matrix, panel):
    matrix = pltpu.with_memory_space_constraint(matrix, pltpu.HBM)
    panel = pltpu.with_memory_space_constraint(panel.T, pltpu.HBM)
    band, base, yj, yc = gathered(matrix, panel)
    return pl.pallas_call(
        update_kernel,
        out_shape=(
            jax.ShapeDtypeStruct((ROWS, COLS), F32),
            jax.ShapeDtypeStruct((WIDTH, WIDTH), F32),
        ),
        in_specs=[pl.BlockSpec(memory_space=pltpu.VMEM)] * 4,
        out_specs=(
            pl.BlockSpec(memory_space=pltpu.HBM),
            pl.BlockSpec(memory_space=pltpu.VMEM),
        ),
        scratch_shapes=[pltpu.VMEM((ROWS, COLS), F32), pltpu.SemaphoreType.DMA((3,))],
        compiler_params=pltpu.CompilerParams(vmem_limit_bytes=40 * 1024 * 1024),
        cost_estimate=pl.CostEstimate(flops=10**8, bytes_accessed=10**7, transcendentals=0),
    )(base, yj, yc, band)


def solution(mesh):
    return jax.shard_map(
        body,
        mesh=mesh,
        in_specs=(P("row", "col"), P("row", None)),
        out_specs=(P("row", "col"), P()),
        check_vma=False,
    )
```

```python
import jax
import jax.numpy as jnp
from jax import lax
from jax.experimental import pallas as pl
from jax.experimental.pallas import tpu as pltpu
from jax.sharding import PartitionSpec as P

F32 = jnp.float32
precise = lax.Precision.HIGHEST
ROWS, COLS, WIDTH = 384, 768, 64
SLAB = 12
HALF = 192


def mm(a, b, ca=1, cb=0):
    return lax.dot_general(
        a, b, (((ca,), (cb,)), ((), ())), precision=precise, preferred_element_type=F32
    )


def halves(x):
    high = x.astype(jnp.bfloat16)
    return high, (x - high.astype(F32)).astype(jnp.bfloat16)


def mm3(a, b):
    (ah, al), (bh, bl) = a, b
    dot = lambda u, v: lax.dot_general(
        u, v, (((1,), (1,)), ((), ())), preferred_element_type=F32
    )
    return dot(ah, bh) + (dot(ah, bl) + dot(al, bh))


def loop(lo, hi, step):
    lax.fori_loop(lo, hi, lambda i, carry: (step(i), carry)[1], 0)


def fold(block):
    rows = block.shape[0] // 2
    return jnp.concatenate([block[:rows], block[rows:]], axis=1)


def unfold(block):
    return jnp.concatenate([block[:, :64], block[:, 64:]], axis=0)


def to_slabs(ref, lead, block):
    folded = fold(block)
    for i in range(16):
        ref[lead + i] = folded[SLAB * i : SLAB * i + SLAB]


def from_slabs(read):
    return unfold(jnp.concatenate([read(i) for i in range(16)], axis=0))


def gather_kernel(
    a_hbm, p_hbm, band_ref, base_ref, yj_ref, yc_ref,
    a_ref, pt_ref, p3, t3, t1, tr, own3, b3, d3, zr, br,
    gh_ref, gh1_ref, gr_ref, gx_ref, hx_ref, gs_ref,
    j_ref, j1_ref, jr_ref,
    gk, hh, ln, rk, lno,
    load_sem, one_send, one_recv,
    gs_sem, gr_sem, hs_sem, ts_sem, tr_sem, bs_sem,
    zs_sem, zr_sem, ys_sem, yr_sem, js_sem, jr_sem, ds_sem, dr_sem,
):
    row = lax.axis_index("row")
    col = lax.axis_index("col")
    chip = row // 2
    core = row % 2
    other = 1 - core
    near = (chip * 2 + other, col)
    swap = (col * 2 + core, chip)

    zs, bs, pp_ref = own3.at[0], own3.at[1], own3.at[2]
    loads = [pltpu.make_async_copy(p_hbm, pt_ref, load_sem.at[0])]
    for b in range(3):
        cut = pl.ds(256 * b, 256)
        loads.append(pltpu.make_async_copy(a_hbm.at[:, cut], a_ref.at[:, cut], load_sem.at[1 + b]))
    for load in loads:
        load.start()

    def peer(d):
        return (chip + d) % 16

    def plane(i):
        return (i * 2 + core, col)

    def remote(src, dst, send, recv, device):
        return pltpu.make_async_remote_copy(
            src_ref=src, dst_ref=dst, send_sem=send, recv_sem=recv,
            device_id=device, device_id_type=pl.DeviceIdType.MESH,
        )

    barrier = pltpu.get_barrier_semaphore()

    def greet(device):
        pl.semaphore_signal(
            barrier, inc=1, device_id=device, device_id_type=pl.DeviceIdType.MESH
        )

    loop(1, 16, lambda d: greet((peer(d) * 2 + core, chip)))

    @pl.when(chip != col)
    def _():
        greet((row, chip))

    loop(1, 16, lambda d: greet(plane(peer(d))))
    greet(near)

    @pl.when(chip > 0)
    def _():
        @pl.when(core == 1)
        def _():
            greet((0, col))

    ring = (col + 8) % 16 - 8
    beside = jnp.where(ring < 0, -ring, ring)

    @pl.when(beside > 0)
    def _():
        @pl.when(beside < 4)
        def _():
            greet((row, 0))

    loads[0].wait()
    pt = pt_ref[...]
    panel = pt.T
    is_first = (row == 0).astype(F32)
    gh_ref[0] = fold(mm(pt, pt, 1, 1))
    gh_ref[1] = fold(panel[:WIDTH]) * is_first
    to_slabs(p3, 0, panel)
    parts = []
    for b in range(3):
        loads[1 + b].wait()
        parts.append(mm(pt, a_ref[:, 256 * b : 256 * b + 256]).T)
    partial = jnp.concatenate(parts, axis=0)
    to_slabs(t3, 0, partial[:ROWS])
    to_slabs(t3, 16, partial[ROWS:])

    @pl.when(col == 0)
    def _():
        to_slabs(br, 0, a_ref[:, :WIDTH])

    @pl.when(row == 0)
    def _():
        first_columns = a_ref[:WIDTH].T
        to_slabs(b3, 0, first_columns[:ROWS])
        to_slabs(b3, 16, first_columns[ROWS:])
        bs[...] = b3[0]

        @pl.when(col == 0)
        def _():
            pl.semaphore_wait(barrier, 52)

        @pl.when(col > 0)
        def _():
            pl.semaphore_wait(barrier, 47)

    @pl.when(row > 0)
    def _():
        @pl.when(col == 0)
        def _():
            @pl.when(chip == 0)
            def _():
                pl.semaphore_wait(barrier, 37)

            @pl.when(chip > 0)
            def _():
                pl.semaphore_wait(barrier, 38)

        @pl.when(col > 0)
        def _():
            @pl.when(chip == col)
            def _():
                pl.semaphore_wait(barrier, 31)

            @pl.when(chip != col)
            def _():
                pl.semaphore_wait(barrier, 32)

    send_t = remote(t3.at[pl.ds(other * 16, 16)], t1, one_send.at[2], one_recv.at[2], near)
    send_t.start()
    send_gh = remote(gh_ref, gh1_ref, one_send.at[0], one_recv.at[0], near)
    send_gh.start()

    send_pp = remote(p3.at[col], pp_ref, one_send.at[1], one_recv.at[1], swap)

    @pl.when(chip != col)
    def _():
        send_pp.start()

    def first_slab(i, k):
        return remote(
            b3.at[k * 16 + i], bs, bs_sem.at[k * 16 + i], one_recv.at[6], (i * 2 + k, col)
        )

    def first_rows_to(z):
        return remote(br, br, ys_sem.at[z], one_recv.at[10], (row, z))


    send_t.wait_recv()
    mine = pl.ds(core * 16, 16)
    t3[mine] = t3[mine] + t1[...]

    def send_part(d):
        i = peer(d)
        remote(t3.at[core * 16 + i], tr.at[chip], ts_sem.at[i], tr_sem.at[chip], plane(i)).start()

    loop(1, 16, send_part)
    tr[chip] = t3[core * 16 + chip]

    send_gh.wait_recv()
    half = pl.ds(pl.multiple_of(core * 16, 8), 16)
    gs_ref[0] = gh_ref[0, half] + gh1_ref[0, half]
    gs_ref[1] = gh_ref[1, half] + gh1_ref[1, half]

    def send_gram(d):
        i = peer(d)
        remote(gs_ref.at[0], gr_ref.at[chip], gs_sem.at[i], gr_sem.at[chip], plane(i)).start()

    def send_head(d):
        i = peer(d)
        remote(gs_ref.at[1], hx_ref, hs_sem.at[i], one_recv.at[5], plane(i)).start()

    loop(1, 16, send_gram)


    gr_ref[chip] = gs_ref[0]


    @pl.when(chip == 0)
    def _():
        loop(1, 16, send_head)

    @pl.when(row == 0)
    def _():
        loop(1, 16, lambda i: first_slab(i, 0).start())
        loop(0, 16, lambda i: first_slab(i, 1).start())

    slot = core * 16 + chip

    def spread(src, dst, send, recv):
        def step(d):
            z = (col + d) % 16
            remote(src, dst.at[chip], send.at[z], recv.at[chip], (col * 2 + core, z)).start()

        loop(1, 16, step)

        @pl.when(chip != col)
        def _():
            step(0)

        @pl.when(chip == col)
        def _():
            dst[chip] = src[...]

    def wait_part(d):
        i = peer(d)
        remote(t3.at[core * 16 + i], tr.at[i], ts_sem.at[i], tr_sem.at[i], plane(i)).wait_recv()

    loop(1, 16, wait_part)
    total = tr[0]
    for i in range(1, 16):
        total = total + tr[i]
    zs[...] = total
    spread(zs, zr, zs_sem, zr_sem)

    def wait_gram(d):
        i = peer(d)
        remote(gs_ref.at[0], gr_ref.at[i], gs_sem.at[i], gr_sem.at[i], plane(i)).wait_recv()

    loop(1, 16, wait_gram)
    total = gr_ref[0]
    for i in range(1, 16):
        total = total + gr_ref[i]

    @pl.when(chip != 0)
    def _():
        remote(gs_ref.at[1], hx_ref, hs_sem.at[0], one_recv.at[5], plane(0)).wait_recv()

    @pl.when(chip == 0)
    def _():
        hx_ref[...] = gs_ref[1]

    gx_ref[0, half] = total
    gx_ref[1, half] = hx_ref[...]
    send_gx = remote(
        gx_ref.at[:, half], gx_ref.at[:, half], one_send.at[4], one_recv.at[4], near
    )
    send_gx.start()


    @pl.when(col == 0)
    def _():
        for z in (1, 15, 2, 14, 3, 13):
            first_rows_to(z).start()

    @pl.when(row > 0)
    def _():
        first_slab(0, 0).wait_recv()

    def first_to(d):
        z = 4 + (col + d) % 9
        return z, remote(bs, br.at[chip], ys_sem.at[z], yr_sem.at[chip], (col * 2 + core, z))

    def send_first(d):
        z, copy = first_to(d)

        @pl.when(chip != col)
        def _():
            copy.start()

        @pl.when(chip == col)
        def _():
            @pl.when(z != col)
            def _():
                copy.start()

            @pl.when(z == col)
            def _():
                br[chip] = bs[...]

    loop(0, 9, send_first)

    send_gx.wait_recv()
    gram = unfold(gx_ref[0])
    head = unfold(gx_ref[1])
    eye = jnp.where(
        lax.broadcasted_iota(jnp.int32, (64, 64), 0)
        == lax.broadcasted_iota(jnp.int32, (64, 64), 1), 1.0, 0.0,
    )
    gk[...] = jnp.concatenate([gram, eye], axis=1)
    hh[...] = jnp.concatenate([head, head.T], axis=1)
    ln[...] = jnp.concatenate([eye, eye], axis=1)

    lane = lax.broadcasted_iota(jnp.int32, (64, 128), 1)
    deep = lax.broadcasted_iota(jnp.int32, (64, 128), 0)
    lane1 = lax.broadcasted_iota(jnp.int32, (1, 128), 1)
    left = lane < 64
    left1 = lane1 < 64

    def pick(x, at, j):
        return jnp.sum(jnp.where(at == j, x, 0.0), axis=1, keepdims=True)

    def inverse_root(x):
        guess = lax.rsqrt(x)
        return guess * (1.5 - 0.5 * x * guess * guess)

    def pair(step):
        j = 2 * step
        i = j + 1
        one, two = pl.ds(j, 1), pl.ds(i, 1)
        g, h, l = gk[...], hh[...], ln[...]
        g1, g2, h1, h2, l1, l2 = gk[one], gk[two], hh[one], hh[two], ln[one], ln[two]
        a, b, d = pick(g1, lane1, j), pick(g1, lane1, i), pick(g2, lane1, i)
        h11, h12 = pick(h1, lane1, j), pick(h1, lane1, i)
        h21, h22 = pick(h2, lane1, j), pick(h2, lane1, i)
        gc1, gc2 = pick(g, lane, j), pick(g, lane, i)
        hc1, hc2 = pick(h, lane, j), pick(h, lane, i)
        mc1, mc2 = pick(h, lane, j + 64), pick(h, lane, i + 64)
        inv1 = inverse_root(a)
        s1, c1, t = g1 * inv1, gc1 * inv1, b * inv1
        rest = d - t * t
        inv2 = inverse_root(rest)
        s2, c2 = (g2 - t * s1) * inv2, (gc2 - t * c1) * inv2
        rk[one] = -s1
        rk[two] = -s2
        gk[...] = g - c1 * s1 - c2 * s2
        turn1 = 1.0 / (h11 + a * inv1)
        m12 = h12 + t
        l21 = h21 * turn1
        turn2 = 1.0 / (h22 - l21 * m12 + rest * inv2)
        lc1, mr1 = hc1 * turn1, mc1 + c1
        lc2, mr2 = (hc2 - lc1 * m12) * turn2, mc2 - mr1 * l21 + c2
        f1 = jnp.where(deep > j, jnp.where(left, lc1, mr1), 0.0)
        f2 = jnp.where(deep > i, jnp.where(left, lc2, mr2), 0.0)
        f21 = jnp.where(left1, l21, m12)
        hl1 = jnp.where(left1, h1 + s1, h1 * turn1)
        h2 = h2 - f21 * hl1
        hl2 = jnp.where(left1, h2 + s2, h2 * turn2)
        ll1 = jnp.where(left1, l1, l1 * turn1)
        l2 = l2 - f21 * ll1
        ll2 = jnp.where(left1, l2, l2 * turn2)
        lno[one] = ll1
        lno[two] = ll2
        hh[...] = h - f1 * hl1 - f2 * hl2
        ln[...] = l - f1 * ll1 - f2 * ll2

    loop(0, 12, pair)

    @pl.when(chip != col)
    def _():
        send_pp.wait_recv()

    @pl.when(chip == col)
    def _():
        pp_ref[...] = p3[col]

    slot = core * 16 + chip

    def share(d):
        i = peer(d)
        return remote(own3, d3.at[slot], ds_sem.at[i], dr_sem.at[chip], plane(i))

    loop(1, 16, lambda d: share(d).start())
    d3[slot] = own3[...]
    loop(12, 32, pair)

    band = jnp.where(
        lax.broadcasted_iota(jnp.int32, (64, 64), 0)
        <= lax.broadcasted_iota(jnp.int32, (64, 64), 1), rk[:, :64], 0.0,
    )
    band_ref[...] = band
    rs = -mm(lno[:, :64], lno[:, 64:], 0, 0)
    s = mm(rk[:, 64:], rs, 0, 0)

    def wait_rows(d):
        i = peer(d)
        to = d3.at[core * 16 + i]
        remote(to, to, ds_sem.at[i], dr_sem.at[i], plane(i)).wait_recv()


    y = jnp.concatenate([panel[:WIDTH] - is_first * band, panel[WIDTH:]], axis=0)
    ys = mm(y, s)
    spread_left = jnp.concatenate([mm(y, s, 1, 1), -mm(y, rs, 1, 1)], axis=1)
    folded_ys = fold(ys)

    def twice(block):
        none = jnp.zeros_like(block)
        return jnp.concatenate(
            [jnp.concatenate([block, none], axis=1), jnp.concatenate([none, block], axis=1)],
            axis=0,
        )

    def stacked(ref):
        return jnp.concatenate([ref[i] for i in range(16)], axis=0)

    twice_s = twice(s)

    @pl.when(beside > 0)
    def _():
        @pl.when(beside < 4)
        def _():
            first_rows_to(0).wait_recv()

    @pl.when(beside > 3)
    def _():
        def wait_first(d):
            i = peer(d)
            remote(bs, br.at[i], ys_sem.at[i], yr_sem.at[i], swap).wait_recv()

        loop(1, 16, wait_first)

        @pl.when(chip != col)
        def _():
            wait_first(0)

    first_part = mm(stacked(br), twice(rs))

    def wait_spread(d):
        i = peer(d)
        remote(zs, zr.at[i], zs_sem.at[i], zr_sem.at[i], swap).wait_recv()

    loop(1, 16, wait_spread)

    @pl.when(chip != col)
    def _():
        wait_spread(0)

    folded_begun = mm(stacked(zr), twice_s) - first_part
    inner = mm(folded_ys, folded_begun, 0, 0)
    inner = inner[:64, :64] + inner[64:, 64:]

    at_row = lax.broadcasted_iota(jnp.int32, (32, 32), 0)
    at_lane = lax.broadcasted_iota(jnp.int32, (32, 32), 1)
    inner = 0.5 * (inner + inner.T)
    corner = inner[32:, 32:]
    mixed = jnp.where(at_row <= at_lane, inner[:32, :32], corner)
    j_ref[:16] = fold(jnp.concatenate([mixed, inner[:32, 32:]], axis=1))
    j_ref[16:, :32] = jnp.sum(jnp.where(at_row == at_lane, corner, 0.0), axis=0, keepdims=True)
    j_ref[16:, 32:] = jnp.zeros((1, 96), F32)
    send_j = remote(j_ref, j1_ref, one_send.at[8], one_recv.at[8], near)
    send_j.start()
    loop(1, 16, wait_rows)
    own = d3.at[mine]
    send_d = remote(own, own, one_send.at[6], one_recv.at[7], near)
    send_d.start()
    send_j.wait_recv()
    jr_ref[chip] = j_ref[...] + j1_ref[...]

    def send_inner(d):
        i = peer(d)
        remote(jr_ref.at[chip], jr_ref.at[chip], js_sem.at[i], jr_sem.at[chip], plane(i)).start()

    def wait_inner(d):
        i = peer(d)
        remote(jr_ref.at[i], jr_ref.at[i], js_sem.at[i], jr_sem.at[i], plane(i)).wait_recv()

    loop(1, 16, send_inner)

    send_d.wait_recv()
    send_d.wait_send()
    rights = [
        jnp.concatenate(
            [from_slabs(lambda i: d3[k * 16 + i, which]) for k in range(2)], axis=0
        )
        for which in range(3)
    ]
    zero_col = (col == 0).astype(F32)
    yc = jnp.concatenate([rights[2][:WIDTH] - zero_col * band, rights[2][WIDTH:]], axis=0)
    yc_ref[...] = yc
    right = jnp.concatenate([rights[0], rights[1], yc], axis=1)
    begun = unfold(folded_begun)
    whole_left = halves(jnp.concatenate([spread_left, begun], axis=1))
    for b in range(3):
        cut = slice(256 * b, 256 * b + 256)
        base_ref[:, cut] = a_ref[:, cut] - mm3(whole_left, halves(right[cut]))

    send_gh.wait_send()
    send_t.wait_send()
    send_gx.wait_send()
    send_j.wait_send()

    @pl.when(chip != col)
    def _():
        send_pp.wait_send()

    def sent(d):
        i = peer(d)
        remote(gs_ref.at[0], gr_ref.at[chip], gs_sem.at[i], gr_sem.at[chip], plane(i)).wait_send()
        remote(t3.at[i], tr.at[chip], ts_sem.at[i], tr_sem.at[chip], plane(i)).wait_send()
        share(d).wait_send()

    loop(1, 16, sent)

    @pl.when(chip == 0)
    def _():
        def head_sent(d):
            i = peer(d)
            remote(gs_ref.at[1], hx_ref, hs_sem.at[i], one_recv.at[5], plane(i)).wait_send()

        loop(1, 16, head_sent)

    @pl.when(row == 0)
    def _():
        loop(1, 16, lambda i: first_slab(i, 0).wait_send())
        loop(0, 16, lambda i: first_slab(i, 1).wait_send())

    @pl.when(col == 0)
    def _():
        for z in (1, 15, 2, 14, 3, 13):
            first_rows_to(z).wait_send()

    def first_sent(d):
        z, copy = first_to(d)

        @pl.when(chip != col)
        def _():
            copy.wait_send()

        @pl.when(chip == col)
        def _():
            @pl.when(z != col)
            def _():
                copy.wait_send()

    loop(0, 9, first_sent)

    def spread_sent(d):
        z = (col + d) % 16
        remote(zs, zr.at[chip], zs_sem.at[z], zr_sem.at[chip], swap).wait_send()

    loop(1, 16, spread_sent)

    @pl.when(chip != col)
    def _():
        spread_sent(0)

    loop(1, 16, wait_inner)
    total = jr_ref[0]
    for i in range(1, 16):
        total = total + jr_ref[i]
    def inner_sent(d):
        i = peer(d)
        remote(jr_ref.at[chip], jr_ref.at[chip], js_sem.at[i], jr_sem.at[chip], plane(i)).wait_send()

    loop(1, 16, inner_sent)
    packed = unfold(total[:16])
    mixed, side = packed[:, :32], packed[:, 32:]
    upper = jnp.where(at_row <= at_lane, mixed, 0.0)
    lower = jnp.where(at_row > at_lane, mixed, 0.0)
    strict = jnp.where(at_row < at_lane, mixed, 0.0)
    corner = lower + lower.T + jnp.where(at_row == at_lane, total[16:, :32], 0.0)
    coupling = jnp.concatenate(
        [
            jnp.concatenate([upper + strict.T, side], axis=1),
            jnp.concatenate([side.T, corner], axis=1),
        ],
        axis=0,
    )
    yj_ref[...] = mm3(halves(y), halves(coupling))


def gathered(matrix, panel):
    dma = pltpu.SemaphoreType.DMA
    vmem = pltpu.VMEM
    slabs = lambda *lead: vmem((*lead, SLAB, 128), F32)
    return pl.pallas_call(
        gather_kernel,
        out_shape=(
            jax.ShapeDtypeStruct((WIDTH, WIDTH), F32),
            jax.ShapeDtypeStruct((ROWS, COLS), F32),
            jax.ShapeDtypeStruct((ROWS, WIDTH), F32),
            jax.ShapeDtypeStruct((COLS, WIDTH), F32),
        ),
        in_specs=[pl.BlockSpec(memory_space=pltpu.HBM)] * 2,
        out_specs=[pl.BlockSpec(memory_space=pltpu.VMEM)] * 4,
        scratch_shapes=[
            vmem((ROWS, COLS), F32),
            vmem((WIDTH, ROWS), F32),
            slabs(16), slabs(32), slabs(16), slabs(16), slabs(3),
            slabs(32), slabs(32, 3), slabs(16), slabs(16),
            vmem((2, 32, 128), F32),
            vmem((2, 32, 128), F32),
            vmem((16, 16, 128), F32),
            vmem((2, 32, 128), F32),
            vmem((16, 128), F32),
            vmem((2, 16, 128), F32),
            vmem((17, 128), F32),
            vmem((17, 128), F32),
            vmem((16, 17, 128), F32),
        ]
        + [vmem((64, 128), F32)] * 5
        + [dma((4,)), dma((10,)), dma((11,))]
        + [dma((16,))] * 5
        + [dma((32,))]
        + [dma((16,))] * 8,
        compiler_params=pltpu.CompilerParams(
            collective_id=0, has_side_effects=True, vmem_limit_bytes=40 * 1024 * 1024
        ),
        cost_estimate=pl.CostEstimate(flops=10**9, bytes_accessed=10**7, transcendentals=0),
    )(matrix, panel)


def update_kernel(base_ref, yj_ref, yc_ref, band_ref, out_hbm, band_out, out, done):
    band_out[...] = band_ref[...]
    yj = halves(yj_ref[...])
    copies = []
    for b in range(3):
        cut = pl.ds(256 * b, 256)
        out[:, cut] = base_ref[:, cut] + mm3(yj, halves(yc_ref[cut]))
        copies.append(pltpu.make_async_copy(out.at[:, cut], out_hbm.at[:, cut], done.at[b]))
        copies[-1].start()
    for copy in copies:
        copy.wait()


def body(matrix, panel):
    matrix = pltpu.with_memory_space_constraint(matrix, pltpu.HBM)
    panel = pltpu.with_memory_space_constraint(panel.T, pltpu.HBM)
    band, base, yj, yc = gathered(matrix, panel)
    return pl.pallas_call(
        update_kernel,
        out_shape=(
            jax.ShapeDtypeStruct((ROWS, COLS), F32),
            jax.ShapeDtypeStruct((WIDTH, WIDTH), F32),
        ),
        in_specs=[pl.BlockSpec(memory_space=pltpu.VMEM)] * 4,
        out_specs=(
            pl.BlockSpec(memory_space=pltpu.HBM),
            pl.BlockSpec(memory_space=pltpu.VMEM),
        ),
        scratch_shapes=[pltpu.VMEM((ROWS, COLS), F32), pltpu.SemaphoreType.DMA((3,))],
        compiler_params=pltpu.CompilerParams(vmem_limit_bytes=40 * 1024 * 1024),
        cost_estimate=pl.CostEstimate(flops=10**8, bytes_accessed=10**7, transcendentals=0),
    )(base, yj, yc, band)


def solution(mesh):
    return jax.shard_map(
        body,
        mesh=mesh,
        in_specs=(P("row", "col"), P("row", None)),
        out_specs=(P("row", "col"), P()),
        check_vma=False,
    )
```

```python
import jax
import jax.numpy as jnp
from jax import lax
from jax.experimental import pallas as pl
from jax.experimental.pallas import tpu as pltpu
from jax.sharding import PartitionSpec as P

F32 = jnp.float32
precise = lax.Precision.HIGHEST
ROWS, COLS, WIDTH = 384, 768, 64
SLAB = 12
HALF = 192


def mm(a, b, ca=1, cb=0):
    return lax.dot_general(
        a, b, (((ca,), (cb,)), ((), ())), precision=precise, preferred_element_type=F32
    )


def halves(x):
    high = x.astype(jnp.bfloat16)
    return high, (x - high.astype(F32)).astype(jnp.bfloat16)


def mm3(a, b):
    (ah, al), (bh, bl) = a, b
    dot = lambda u, v: lax.dot_general(
        u, v, (((1,), (1,)), ((), ())), preferred_element_type=F32
    )
    return dot(ah, bh) + (dot(ah, bl) + dot(al, bh))


def loop(lo, hi, step):
    unroll = 5 if hi - lo == 15 else 1
    lax.fori_loop(lo, hi, lambda i, carry: (step(i), carry)[1], 0, unroll=unroll)


def fold(block):
    rows = block.shape[0] // 2
    return jnp.concatenate([block[:rows], block[rows:]], axis=1)


def unfold(block):
    return jnp.concatenate([block[:, :64], block[:, 64:]], axis=0)


def to_slabs(ref, lead, block):
    folded = fold(block)
    for i in range(16):
        ref[lead + i] = folded[SLAB * i : SLAB * i + SLAB]


def from_slabs(read):
    return unfold(jnp.concatenate([read(i) for i in range(16)], axis=0))


def gather_kernel(
    a_hbm, p_hbm, band_ref, base_ref, yj_ref, yc_ref,
    a_ref, pt_ref, p3, t3, t1, tr, own3, b3, d3, zr, br,
    gh_ref, gh1_ref, gr_ref, gx_ref, hx_ref, gs_ref,
    j_ref, j1_ref, jr_ref,
    gk, hh, ln, rk, lno,
    load_sem, one_send, one_recv,
    gs_sem, gr_sem, hs_sem, ts_sem, tr_sem, bs_sem,
    zs_sem, zr_sem, ys_sem, yr_sem, js_sem, jr_sem, ds_sem, dr_sem,
):
    row = lax.axis_index("row")
    col = lax.axis_index("col")
    chip = row // 2
    core = row % 2
    other = 1 - core
    near = (chip * 2 + other, col)
    swap = (col * 2 + core, chip)

    zs, bs, pp_ref = own3.at[0], own3.at[1], own3.at[2]
    loads = [pltpu.make_async_copy(p_hbm, pt_ref, load_sem.at[0])]
    for b in range(3):
        cut = pl.ds(256 * b, 256)
        loads.append(pltpu.make_async_copy(a_hbm.at[:, cut], a_ref.at[:, cut], load_sem.at[1 + b]))
    for load in loads:
        load.start()

    def peer(d):
        return (chip + d) % 16

    def plane(i):
        return (i * 2 + core, col)

    def remote(src, dst, send, recv, device):
        return pltpu.make_async_remote_copy(
            src_ref=src, dst_ref=dst, send_sem=send, recv_sem=recv,
            device_id=device, device_id_type=pl.DeviceIdType.MESH,
        )

    barrier = pltpu.get_barrier_semaphore()

    def greet(device):
        pl.semaphore_signal(
            barrier, inc=1, device_id=device, device_id_type=pl.DeviceIdType.MESH
        )

    loop(1, 16, lambda d: greet((peer(d) * 2 + core, chip)))

    @pl.when(chip != col)
    def _():
        greet((row, chip))

    loop(1, 16, lambda d: greet(plane(peer(d))))
    greet(near)

    @pl.when(chip > 0)
    def _():
        @pl.when(core == 1)
        def _():
            greet((0, col))

    ring = (col + 8) % 16 - 8
    beside = jnp.where(ring < 0, -ring, ring)

    @pl.when(beside > 0)
    def _():
        @pl.when(beside < 4)
        def _():
            greet((row, 0))

    loads[0].wait()
    pt = pt_ref[...]
    panel = pt.T
    is_first = (row == 0).astype(F32)
    gh_ref[0] = fold(mm(pt, pt, 1, 1))
    gh_ref[1] = fold(panel[:WIDTH]) * is_first
    to_slabs(p3, 0, panel)
    parts = []
    for b in range(3):
        loads[1 + b].wait()
        parts.append(mm(pt, a_ref[:, 256 * b : 256 * b + 256]).T)
    partial = jnp.concatenate(parts, axis=0)
    to_slabs(t3, 0, partial[:ROWS])
    to_slabs(t3, 16, partial[ROWS:])

    @pl.when(col == 0)
    def _():
        to_slabs(br, 0, a_ref[:, :WIDTH])

    @pl.when(row == 0)
    def _():
        first_columns = a_ref[:WIDTH].T
        to_slabs(b3, 0, first_columns[:ROWS])
        to_slabs(b3, 16, first_columns[ROWS:])
        bs[...] = b3[0]

        @pl.when(col == 0)
        def _():
            pl.semaphore_wait(barrier, 52)

        @pl.when(col > 0)
        def _():
            pl.semaphore_wait(barrier, 47)

    @pl.when(row > 0)
    def _():
        @pl.when(col == 0)
        def _():
            @pl.when(chip == 0)
            def _():
                pl.semaphore_wait(barrier, 37)

            @pl.when(chip > 0)
            def _():
                pl.semaphore_wait(barrier, 38)

        @pl.when(col > 0)
        def _():
            @pl.when(chip == col)
            def _():
                pl.semaphore_wait(barrier, 31)

            @pl.when(chip != col)
            def _():
                pl.semaphore_wait(barrier, 32)

    send_t = remote(t3.at[pl.ds(other * 16, 16)], t1, one_send.at[2], one_recv.at[2], near)
    send_t.start()
    send_gh = remote(gh_ref, gh1_ref, one_send.at[0], one_recv.at[0], near)
    send_gh.start()

    send_pp = remote(p3.at[col], pp_ref, one_send.at[1], one_recv.at[1], swap)

    @pl.when(chip != col)
    def _():
        send_pp.start()

    def first_slab(i, k):
        return remote(
            b3.at[k * 16 + i], bs, bs_sem.at[k * 16 + i], one_recv.at[6], (i * 2 + k, col)
        )

    def first_rows_to(z):
        return remote(br, br, ys_sem.at[z], one_recv.at[10], (row, z))


    send_t.wait_recv()
    mine = pl.ds(core * 16, 16)
    t3[mine] = t3[mine] + t1[...]

    def send_part(d):
        i = peer(d)
        remote(t3.at[core * 16 + i], tr.at[chip], ts_sem.at[i], tr_sem.at[chip], plane(i)).start()

    loop(1, 16, send_part)
    tr[chip] = t3[core * 16 + chip]

    send_gh.wait_recv()
    half = pl.ds(pl.multiple_of(core * 16, 8), 16)
    gs_ref[0] = gh_ref[0, half] + gh1_ref[0, half]
    gs_ref[1] = gh_ref[1, half] + gh1_ref[1, half]

    def send_gram(d):
        i = peer(d)
        remote(gs_ref.at[0], gr_ref.at[chip], gs_sem.at[i], gr_sem.at[chip], plane(i)).start()

    def send_head(d):
        i = peer(d)
        remote(gs_ref.at[1], hx_ref, hs_sem.at[i], one_recv.at[5], plane(i)).start()

    loop(1, 16, send_gram)


    gr_ref[chip] = gs_ref[0]


    @pl.when(chip == 0)
    def _():
        loop(1, 16, send_head)

    @pl.when(row == 0)
    def _():
        loop(1, 16, lambda i: first_slab(i, 0).start())
        loop(0, 16, lambda i: first_slab(i, 1).start())

    slot = core * 16 + chip

    def spread(src, dst, send, recv):
        def step(d):
            z = (col + d) % 16
            remote(src, dst.at[chip], send.at[z], recv.at[chip], (col * 2 + core, z)).start()

        loop(1, 16, step)

        @pl.when(chip != col)
        def _():
            step(0)

        @pl.when(chip == col)
        def _():
            dst[chip] = src[...]

    def wait_part(d):
        i = peer(d)
        remote(t3.at[core * 16 + i], tr.at[i], ts_sem.at[i], tr_sem.at[i], plane(i)).wait_recv()

    loop(1, 16, wait_part)
    total = tr[0]
    for i in range(1, 16):
        total = total + tr[i]
    zs[...] = total
    spread(zs, zr, zs_sem, zr_sem)

    def wait_gram(d):
        i = peer(d)
        remote(gs_ref.at[0], gr_ref.at[i], gs_sem.at[i], gr_sem.at[i], plane(i)).wait_recv()

    loop(1, 16, wait_gram)
    total = gr_ref[0]
    for i in range(1, 16):
        total = total + gr_ref[i]

    @pl.when(chip != 0)
    def _():
        remote(gs_ref.at[1], hx_ref, hs_sem.at[0], one_recv.at[5], plane(0)).wait_recv()

    @pl.when(chip == 0)
    def _():
        hx_ref[...] = gs_ref[1]

    gx_ref[0, half] = total
    gx_ref[1, half] = hx_ref[...]
    send_gx = remote(
        gx_ref.at[:, half], gx_ref.at[:, half], one_send.at[4], one_recv.at[4], near
    )
    send_gx.start()


    @pl.when(col == 0)
    def _():
        for z in (1, 15, 2, 14, 3, 13):
            first_rows_to(z).start()

    @pl.when(row > 0)
    def _():
        first_slab(0, 0).wait_recv()

    def first_to(d):
        z = 4 + (col + d) % 9
        return z, remote(bs, br.at[chip], ys_sem.at[z], yr_sem.at[chip], (col * 2 + core, z))

    def send_first(d):
        z, copy = first_to(d)

        @pl.when(chip != col)
        def _():
            copy.start()

        @pl.when(chip == col)
        def _():
            @pl.when(z != col)
            def _():
                copy.start()

            @pl.when(z == col)
            def _():
                br[chip] = bs[...]

    loop(0, 9, send_first)

    send_gx.wait_recv()
    gram = unfold(gx_ref[0])
    head = unfold(gx_ref[1])
    eye = jnp.where(
        lax.broadcasted_iota(jnp.int32, (64, 64), 0)
        == lax.broadcasted_iota(jnp.int32, (64, 64), 1), 1.0, 0.0,
    )
    gk[...] = jnp.concatenate([gram, eye], axis=1)
    hh[...] = jnp.concatenate([head, head.T], axis=1)
    ln[...] = jnp.concatenate([eye, eye], axis=1)

    lane = lax.broadcasted_iota(jnp.int32, (64, 128), 1)
    deep = lax.broadcasted_iota(jnp.int32, (64, 128), 0)
    lane1 = lax.broadcasted_iota(jnp.int32, (1, 128), 1)
    left = lane < 64
    left1 = lane1 < 64

    def pick(x, at, j):
        return jnp.sum(jnp.where(at == j, x, 0.0), axis=1, keepdims=True)

    def inverse_root(x):
        guess = lax.rsqrt(x)
        return guess * (1.5 - 0.5 * x * guess * guess)

    def pair(step):
        j = 2 * step
        i = j + 1
        one, two = pl.ds(j, 1), pl.ds(i, 1)
        g, h, l = gk[...], hh[...], ln[...]
        g1, g2, h1, h2, l1, l2 = gk[one], gk[two], hh[one], hh[two], ln[one], ln[two]
        a, b, d = pick(g1, lane1, j), pick(g1, lane1, i), pick(g2, lane1, i)
        h11, h12 = pick(h1, lane1, j), pick(h1, lane1, i)
        h21, h22 = pick(h2, lane1, j), pick(h2, lane1, i)
        gc1, gc2 = pick(g, lane, j), pick(g, lane, i)
        hc1, hc2 = pick(h, lane, j), pick(h, lane, i)
        mc1, mc2 = pick(h, lane, j + 64), pick(h, lane, i + 64)
        inv1 = inverse_root(a)
        s1, c1, t = g1 * inv1, gc1 * inv1, b * inv1
        rest = d - t * t
        inv2 = inverse_root(rest)
        s2, c2 = (g2 - t * s1) * inv2, (gc2 - t * c1) * inv2
        rk[one] = -s1
        rk[two] = -s2
        gk[...] = g - c1 * s1 - c2 * s2
        turn1 = 1.0 / (h11 + a * inv1)
        m12 = h12 + t
        l21 = h21 * turn1
        turn2 = 1.0 / (h22 - l21 * m12 + rest * inv2)
        lc1, mr1 = hc1 * turn1, mc1 + c1
        lc2, mr2 = (hc2 - lc1 * m12) * turn2, mc2 - mr1 * l21 + c2
        f1 = jnp.where(deep > j, jnp.where(left, lc1, mr1), 0.0)
        f2 = jnp.where(deep > i, jnp.where(left, lc2, mr2), 0.0)
        f21 = jnp.where(left1, l21, m12)
        hl1 = jnp.where(left1, h1 + s1, h1 * turn1)
        h2 = h2 - f21 * hl1
        hl2 = jnp.where(left1, h2 + s2, h2 * turn2)
        ll1 = jnp.where(left1, l1, l1 * turn1)
        l2 = l2 - f21 * ll1
        ll2 = jnp.where(left1, l2, l2 * turn2)
        lno[one] = ll1
        lno[two] = ll2
        hh[...] = h - f1 * hl1 - f2 * hl2
        ln[...] = l - f1 * ll1 - f2 * ll2

    loop(0, 12, pair)

    @pl.when(chip != col)
    def _():
        send_pp.wait_recv()

    @pl.when(chip == col)
    def _():
        pp_ref[...] = p3[col]

    slot = core * 16 + chip

    def share(d):
        i = peer(d)
        return remote(own3, d3.at[slot], ds_sem.at[i], dr_sem.at[chip], plane(i))

    loop(1, 16, lambda d: share(d).start())
    d3[slot] = own3[...]
    loop(12, 32, pair)

    band = jnp.where(
        lax.broadcasted_iota(jnp.int32, (64, 64), 0)
        <= lax.broadcasted_iota(jnp.int32, (64, 64), 1), rk[:, :64], 0.0,
    )
    band_ref[...] = band
    rs = -mm(lno[:, :64], lno[:, 64:], 0, 0)
    s = mm(rk[:, 64:], rs, 0, 0)

    def wait_rows(d):
        i = peer(d)
        to = d3.at[core * 16 + i]
        remote(to, to, ds_sem.at[i], dr_sem.at[i], plane(i)).wait_recv()


    y = jnp.concatenate([panel[:WIDTH] - is_first * band, panel[WIDTH:]], axis=0)
    ys = mm(y, s)
    spread_left = jnp.concatenate([mm(y, s, 1, 1), -mm(y, rs, 1, 1)], axis=1)
    folded_ys = fold(ys)

    def twice(block):
        none = jnp.zeros_like(block)
        return jnp.concatenate(
            [jnp.concatenate([block, none], axis=1), jnp.concatenate([none, block], axis=1)],
            axis=0,
        )

    def stacked(ref):
        return jnp.concatenate([ref[i] for i in range(16)], axis=0)

    twice_s = twice(s)

    @pl.when(beside > 0)
    def _():
        @pl.when(beside < 4)
        def _():
            first_rows_to(0).wait_recv()

    @pl.when(beside > 3)
    def _():
        def wait_first(d):
            i = peer(d)
            remote(bs, br.at[i], ys_sem.at[i], yr_sem.at[i], swap).wait_recv()

        loop(1, 16, wait_first)

        @pl.when(chip != col)
        def _():
            wait_first(0)

    first_part = mm(stacked(br), twice(rs))

    def wait_spread(d):
        i = peer(d)
        remote(zs, zr.at[i], zs_sem.at[i], zr_sem.at[i], swap).wait_recv()

    loop(1, 16, wait_spread)

    @pl.when(chip != col)
    def _():
        wait_spread(0)

    folded_begun = mm(stacked(zr), twice_s) - first_part
    inner = mm(folded_ys, folded_begun, 0, 0)
    inner = inner[:64, :64] + inner[64:, 64:]

    at_row = lax.broadcasted_iota(jnp.int32, (32, 32), 0)
    at_lane = lax.broadcasted_iota(jnp.int32, (32, 32), 1)
    inner = 0.5 * (inner + inner.T)
    corner = inner[32:, 32:]
    mixed = jnp.where(at_row <= at_lane, inner[:32, :32], corner)
    j_ref[:16] = fold(jnp.concatenate([mixed, inner[:32, 32:]], axis=1))
    j_ref[16:, :32] = jnp.sum(jnp.where(at_row == at_lane, corner, 0.0), axis=0, keepdims=True)
    j_ref[16:, 32:] = jnp.zeros((1, 96), F32)
    send_j = remote(j_ref, j1_ref, one_send.at[8], one_recv.at[8], near)
    send_j.start()
    loop(1, 16, wait_rows)
    own = d3.at[mine]
    send_d = remote(own, own, one_send.at[6], one_recv.at[7], near)
    send_d.start()
    send_j.wait_recv()
    jr_ref[chip] = j_ref[...] + j1_ref[...]

    def send_inner(d):
        i = peer(d)
        remote(jr_ref.at[chip], jr_ref.at[chip], js_sem.at[i], jr_sem.at[chip], plane(i)).start()

    def wait_inner(d):
        i = peer(d)
        remote(jr_ref.at[i], jr_ref.at[i], js_sem.at[i], jr_sem.at[i], plane(i)).wait_recv()

    loop(1, 16, send_inner)

    send_d.wait_recv()
    send_d.wait_send()
    rights = [
        jnp.concatenate(
            [from_slabs(lambda i: d3[k * 16 + i, which]) for k in range(2)], axis=0
        )
        for which in range(3)
    ]
    zero_col = (col == 0).astype(F32)
    yc = jnp.concatenate([rights[2][:WIDTH] - zero_col * band, rights[2][WIDTH:]], axis=0)
    yc_ref[...] = yc
    right = jnp.concatenate([rights[0], rights[1], yc], axis=1)
    begun = unfold(folded_begun)
    whole_left = halves(jnp.concatenate([spread_left, begun], axis=1))
    for b in range(3):
        cut = slice(256 * b, 256 * b + 256)
        base_ref[:, cut] = a_ref[:, cut] - mm3(whole_left, halves(right[cut]))

    send_gh.wait_send()
    send_t.wait_send()
    send_gx.wait_send()
    send_j.wait_send()

    @pl.when(chip != col)
    def _():
        send_pp.wait_send()

    def sent(d):
        i = peer(d)
        remote(gs_ref.at[0], gr_ref.at[chip], gs_sem.at[i], gr_sem.at[chip], plane(i)).wait_send()
        remote(t3.at[i], tr.at[chip], ts_sem.at[i], tr_sem.at[chip], plane(i)).wait_send()
        share(d).wait_send()

    loop(1, 16, sent)

    @pl.when(chip == 0)
    def _():
        def head_sent(d):
            i = peer(d)
            remote(gs_ref.at[1], hx_ref, hs_sem.at[i], one_recv.at[5], plane(i)).wait_send()

        loop(1, 16, head_sent)

    @pl.when(row == 0)
    def _():
        loop(1, 16, lambda i: first_slab(i, 0).wait_send())
        loop(0, 16, lambda i: first_slab(i, 1).wait_send())

    @pl.when(col == 0)
    def _():
        for z in (1, 15, 2, 14, 3, 13):
            first_rows_to(z).wait_send()

    def first_sent(d):
        z, copy = first_to(d)

        @pl.when(chip != col)
        def _():
            copy.wait_send()

        @pl.when(chip == col)
        def _():
            @pl.when(z != col)
            def _():
                copy.wait_send()

    loop(0, 9, first_sent)

    def spread_sent(d):
        z = (col + d) % 16
        remote(zs, zr.at[chip], zs_sem.at[z], zr_sem.at[chip], swap).wait_send()

    loop(1, 16, spread_sent)

    @pl.when(chip != col)
    def _():
        spread_sent(0)

    loop(1, 16, wait_inner)
    total = jr_ref[0]
    for i in range(1, 16):
        total = total + jr_ref[i]
    def inner_sent(d):
        i = peer(d)
        remote(jr_ref.at[chip], jr_ref.at[chip], js_sem.at[i], jr_sem.at[chip], plane(i)).wait_send()

    loop(1, 16, inner_sent)
    packed = unfold(total[:16])
    mixed, side = packed[:, :32], packed[:, 32:]
    upper = jnp.where(at_row <= at_lane, mixed, 0.0)
    lower = jnp.where(at_row > at_lane, mixed, 0.0)
    strict = jnp.where(at_row < at_lane, mixed, 0.0)
    corner = lower + lower.T + jnp.where(at_row == at_lane, total[16:, :32], 0.0)
    coupling = jnp.concatenate(
        [
            jnp.concatenate([upper + strict.T, side], axis=1),
            jnp.concatenate([side.T, corner], axis=1),
        ],
        axis=0,
    )
    yj_ref[...] = mm3(halves(y), halves(coupling))


def gathered(matrix, panel):
    dma = pltpu.SemaphoreType.DMA
    vmem = pltpu.VMEM
    slabs = lambda *lead: vmem((*lead, SLAB, 128), F32)
    return pl.pallas_call(
        gather_kernel,
        out_shape=(
            jax.ShapeDtypeStruct((WIDTH, WIDTH), F32),
            jax.ShapeDtypeStruct((ROWS, COLS), F32),
            jax.ShapeDtypeStruct((ROWS, WIDTH), F32),
            jax.ShapeDtypeStruct((COLS, WIDTH), F32),
        ),
        in_specs=[pl.BlockSpec(memory_space=pltpu.HBM)] * 2,
        out_specs=[pl.BlockSpec(memory_space=pltpu.VMEM)] * 4,
        scratch_shapes=[
            vmem((ROWS, COLS), F32),
            vmem((WIDTH, ROWS), F32),
            slabs(16), slabs(32), slabs(16), slabs(16), slabs(3),
            slabs(32), slabs(32, 3), slabs(16), slabs(16),
            vmem((2, 32, 128), F32),
            vmem((2, 32, 128), F32),
            vmem((16, 16, 128), F32),
            vmem((2, 32, 128), F32),
            vmem((16, 128), F32),
            vmem((2, 16, 128), F32),
            vmem((17, 128), F32),
            vmem((17, 128), F32),
            vmem((16, 17, 128), F32),
        ]
        + [vmem((64, 128), F32)] * 5
        + [dma((4,)), dma((10,)), dma((11,))]
        + [dma((16,))] * 5
        + [dma((32,))]
        + [dma((16,))] * 8,
        compiler_params=pltpu.CompilerParams(
            collective_id=0, has_side_effects=True, vmem_limit_bytes=40 * 1024 * 1024
        ),
        cost_estimate=pl.CostEstimate(flops=10**9, bytes_accessed=10**7, transcendentals=0),
    )(matrix, panel)


def update_kernel(base_ref, yj_ref, yc_ref, band_ref, out_hbm, band_out, out, done):
    band_out[...] = band_ref[...]
    yj = halves(yj_ref[...])
    copies = []
    for b in range(3):
        cut = pl.ds(256 * b, 256)
        out[:, cut] = base_ref[:, cut] + mm3(yj, halves(yc_ref[cut]))
        copies.append(pltpu.make_async_copy(out.at[:, cut], out_hbm.at[:, cut], done.at[b]))
        copies[-1].start()
    for copy in copies:
        copy.wait()


def body(matrix, panel):
    matrix = pltpu.with_memory_space_constraint(matrix, pltpu.HBM)
    panel = pltpu.with_memory_space_constraint(panel.T, pltpu.HBM)
    band, base, yj, yc = gathered(matrix, panel)
    return pl.pallas_call(
        update_kernel,
        out_shape=(
            jax.ShapeDtypeStruct((ROWS, COLS), F32),
            jax.ShapeDtypeStruct((WIDTH, WIDTH), F32),
        ),
        in_specs=[pl.BlockSpec(memory_space=pltpu.VMEM)] * 4,
        out_specs=(
            pl.BlockSpec(memory_space=pltpu.HBM),
            pl.BlockSpec(memory_space=pltpu.VMEM),
        ),
        scratch_shapes=[pltpu.VMEM((ROWS, COLS), F32), pltpu.SemaphoreType.DMA((3,))],
        compiler_params=pltpu.CompilerParams(vmem_limit_bytes=40 * 1024 * 1024),
        cost_estimate=pl.CostEstimate(flops=10**8, bytes_accessed=10**7, transcendentals=0),
    )(base, yj, yc, band)


def solution(mesh):
    return jax.shard_map(
        body,
        mesh=mesh,
        in_specs=(P("row", "col"), P("row", None)),
        out_specs=(P("row", "col"), P()),
        check_vma=False,
    )
```
